512 devices in a mesh: seq: 64 (over x, z), tp: 8 (over y, core).
Axes of the slice: x: 4, y: 4, z: 16, core: 2. Of those that a mesh axis runs over, the one named last changes fastest.
Arguments:
- streams: bfloat16 [3, 8192, 16384], P(None, 'tp', 'seq'), may hold values from -6 to 6
- short_taps: float32 [3, 8192, 7], P(None, 'tp'), may hold values from -2 to 2
- long_taps: float32 [512, 128], P('tp'), may hold values from -0.5 to 0.5
- doc_marks: int32 [16384], P('seq'), may hold values 0 or 1
- upstream: bfloat16 [8192, 16384], P('tp', 'seq'), may hold values from -6 to 6
Outputs:
- mixed_out: bfloat16 [8192, 16384], P('tp', 'seq')
- grad_streams: bfloat16 [3, 8192, 16384], P(None, 'tp', 'seq')
- grad_long: float32 [512, 128], P('tp')
- grad_short: float32 [3, 8192, 7], P(None, 'tp')
The draws below stay inside these ranges and needn't reach their ends.
All inputs are finite; a program needn't handle non-finite values. No bound on the sum of `doc_marks` on one device may be relied on, other than what follows from the above.
Results may differ from the reference program's by a relative error of at most 0.015.
Values may be sent and summed in bfloat16 or wider, within the bound.
No kernel may reach another device: no remote copies, remote signals or barrier semaphores. Data moves between devices by JAX's collectives and lax.ppermute only.
A program may use at most 64 MiB of HBM per device.

```python
import jax
import jax.numpy as jnp
from jax import lax

D = 8192
GROUP = 16
TAPS = 128
SHORT = 7
TOK_DEV = 256
GROUPS = 512
TOKENS = 16384


def plant(entries, own_key, smallest, largest):
    longest = entries.shape.index(max(entries.shape))
    spots = []
    for shift in (0, 1):
        where = [jax.random.randint(jax.random.fold_in(own_key, axis), (), 0, length) for axis, length in enumerate(entries.shape)]
        where[longest] = (where[longest] + shift) % entries.shape[longest]
        spots.append(tuple(where))
    return entries.at[spots[0]].set(smallest).at[spots[1]].set(largest)


def steps_of(stream_key, dims, pieces, least, top_value):
    level = 1.0
    for dim, blocks in pieces:
        steps = jax.random.uniform(jax.random.fold_in(jax.random.fold_in(stream_key, 6), dim), (blocks,), jnp.float32, least / len(pieces), top_value / len(pieces))
        level = level * jnp.repeat(jnp.exp(steps), dims[dim] // blocks).reshape((-1,) + (1,) * (len(dims) - 1 - dim))
    return level


def noise(stream_key, shape, scale, most, split=(), kind=jnp.bfloat16):
    values = jax.random.normal(stream_key, shape, jnp.float32) * scale
    if len(split) > 0:
        values = steps_of(stream_key, shape, split, -0.22, 0.18) * values
    return jnp.clip(values, min=-most, max=most).astype(kind)


def setup_inputs(seed: int = 0) -> dict:
    streams_of = jax.random.split(jax.random.key(seed), 6)
    streams = noise(streams_of[0], (3, D, TOKENS), 1.0, 6.0, ((1, 8), (2, 64)))
    short_taps = noise(streams_of[1], (3, D, SHORT), SHORT ** -0.5, 2.0, ((1, 8),), jnp.float32)
    long_taps = noise(streams_of[2], (GROUPS, TAPS), TAPS ** -0.5, 0.5, ((0, 8),), jnp.float32)
    doc_marks = plant((jax.random.randint(streams_of[3], (TOKENS,), 0, 96) < 1).astype(jnp.int32), jax.random.fold_in(streams_of[3], 1), 0, 1)
    upstream = noise(streams_of[4], (D, TOKENS), 1.0, 6.0, ((0, 8), (1, 64)))
    return dict(streams=streams, short_taps=short_taps, long_taps=long_taps, doc_marks=doc_marks, upstream=upstream)


def settle(value):
    return lax.optimization_barrier(value)

def band_table(filt, rows, width, forward):
    count = filt.shape[0]
    taps = filt.shape[1]
    if forward:
        base = jnp.concatenate([jnp.zeros((count, 1), jnp.float32), filt[:, ::-1], jnp.zeros((count, width - taps), jnp.float32)], axis=1)
    else:
        base = jnp.concatenate([filt, jnp.zeros((count, width + 1 - taps), jnp.float32)], axis=1)
    tiled = jnp.tile(base, (1, rows))[:, :rows * width]
    return tiled.reshape(count, rows, width)

def diagonal_sums(product, taps):
    count, rows, width = product.shape
    flat = jnp.pad(product.reshape(count, rows * width), ((0, 0), (0, rows)))
    folded = lax.optimization_barrier(jnp.sum(flat.reshape(count, rows, width + 1), axis=1))
    return folded[:, 1:taps + 1][:, ::-1]

def reference(streams, short_taps, long_taps, doc_marks, upstream):
    length = streams.shape[2]
    chan = streams.shape[1]
    edge = SHORT - 1
    places = jnp.arange(length, dtype=jnp.int32)
    starts = lax.cummax(jnp.where(doc_marks == 1, places, -1), axis=0)
    raw = jnp.pad(streams, ((0, 0), (0, 0), (edge, 0)))
    feats = []
    for index in range(3):
        total = jnp.zeros((chan, length), jnp.float32)
        for lag in range(SHORT):
            keep = (places - lag >= starts).astype(jnp.float32)
            piece = raw[index, :, edge - lag:edge - lag + length].astype(jnp.float32)
            total = total + short_taps[index, :, lag:lag + 1] * piece * keep
        feats.append(settle(total.astype(jnp.bfloat16)))
    feat_q, feat_k, feat_v = feats
    mixed = settle((feat_k.astype(jnp.float32) * feat_v.astype(jnp.float32)).astype(jnp.bfloat16))
    gate_grad = settle((upstream.astype(jnp.float32) * feat_q.astype(jnp.float32)).astype(jnp.bfloat16))
    filt = settle(long_taps.astype(jnp.bfloat16)).astype(jnp.float32)
    width = TOK_DEV + TAPS
    forward_base = band_table(filt, TOK_DEV, width, True)
    backward_base = band_table(filt, TOK_DEV, width, False)
    mixed_pad = jnp.pad(mixed, ((0, 0), (TAPS, 0)))
    gate_pad = jnp.pad(gate_grad, ((0, 0), (0, TAPS)))
    starts_pad = jnp.pad(starts, (0, TAPS))
    rows = jnp.arange(TOK_DEV, dtype=jnp.int32)[:, None]
    cols = jnp.arange(width, dtype=jnp.int32)[None, :]
    lag_grid = cols - rows
    band = ((lag_grid >= 1) & (lag_grid <= TAPS)).astype(jnp.float32)

    def block_step(block):
        first = block * TOK_DEV
        mixed_win = lax.dynamic_slice_in_dim(mixed_pad, first, width, 1).astype(jnp.float32).reshape(GROUPS, GROUP, width)
        gate_win = lax.dynamic_slice_in_dim(gate_pad, first, width, 1).astype(jnp.float32).reshape(GROUPS, GROUP, width)
        gate_part = gate_win[:, :, :TOK_DEV]
        own_starts = lax.dynamic_slice_in_dim(starts, first, TOK_DEV)
        back_starts = lax.dynamic_slice_in_dim(starts_pad, first, width)
        fwd_doc = (first - TAPS + cols >= own_starts[:, None]).astype(jnp.float32)
        back_doc = (first + rows >= back_starts[None, :]).astype(jnp.float32)
        conv = jnp.einsum('gcj,gtj->gct', mixed_win, forward_base * fwd_doc)
        back = jnp.einsum('gct,git->gci', gate_win, backward_base * back_doc)
        product = jnp.einsum('gct,gcj->gtj', gate_part, mixed_win) * (fwd_doc * band)
        return (conv.reshape(chan, TOK_DEV), back.reshape(chan, TOK_DEV), diagonal_sums(product, TAPS))
    blocks = jnp.arange(length // TOK_DEV, dtype=jnp.int32)
    conv, back, filt_parts = lax.map(block_step, blocks)
    conv = jnp.transpose(conv, (1, 0, 2)).reshape(chan, length)
    back = jnp.transpose(back, (1, 0, 2)).reshape(chan, length)
    filt_grad = lax.optimization_barrier(jnp.sum(filt_parts, axis=0))
    mixed_out = (feat_q.astype(jnp.float32) * conv).astype(jnp.bfloat16)
    grad_q = settle((upstream.astype(jnp.float32) * conv).astype(jnp.bfloat16))
    grad_k = settle((back * feat_v.astype(jnp.float32)).astype(jnp.bfloat16))
    grad_v = settle((back * feat_k.astype(jnp.float32)).astype(jnp.bfloat16))
    feat_grad = [grad_q, grad_k, grad_v]
    starts_tail = jnp.pad(starts, (0, edge))
    grads = []
    short_rows = []
    for index in range(3):
        grad_pad = jnp.pad(feat_grad[index], ((0, 0), (0, edge))).astype(jnp.float32)
        total = jnp.zeros((chan, length), jnp.float32)
        columns = []
        for lag in range(SHORT):
            keep = (places >= starts_tail[lag:lag + length]).astype(jnp.float32)
            total = total + short_taps[index, :, lag:lag + 1] * grad_pad[:, lag:lag + length] * keep
            valid = (places - lag >= starts).astype(jnp.float32)
            piece = raw[index, :, edge - lag:edge - lag + length].astype(jnp.float32)
            columns.append(lax.optimization_barrier(jnp.sum(feat_grad[index].astype(jnp.float32) * piece * valid, axis=1)))
        grads.append(total.astype(jnp.bfloat16))
        short_rows.append(jnp.stack(columns, axis=1))
    grad_streams = jnp.stack(grads)
    short_grad = jnp.stack(short_rows)
    count = GROUPS * TAPS + 3 * D * SHORT
    mean_square = (jnp.sum(filt_grad * filt_grad) + jnp.sum(short_grad * short_grad)) / count
    scale = jnp.minimum(1.0, 1.0 / jnp.sqrt(mean_square + 1e-06))
    return (mixed_out, grad_streams, filt_grad * scale, short_grad * scale)
```

```python
import functools

import jax
import jax.numpy as jnp
from jax import lax
from jax.experimental import pallas as pl
from jax.experimental.pallas import tpu as pltpu
from jax.sharding import Mesh
from jax.sharding import PartitionSpec as P

BF = jnp.bfloat16
F32 = jnp.float32
SEQ = ("x", "zh", "zl")
TP = ("y", "c")
CUBE = ("x", "zl")
TILE = 128
EDGE_ROWS = 8
BLOCK = 256
LIMIT = 56 * 1024 * 1024


def nt(left, right):
    return lax.dot_general(left, right, (((1,), (1,)), ((), ())), preferred_element_type=F32)


def nn(left, right):
    return lax.dot_general(left, right, (((1,), (0,)), ((), ())), preferred_element_type=F32)


def segments(marks_ref):
    tok = marks_ref.shape[1]
    row = lax.broadcasted_iota(jnp.int32, (tok, tok), 0)
    col = lax.broadcasted_iota(jnp.int32, (tok, tok), 1)
    lower = jnp.where(col <= row, 1.0, 0.0).astype(BF)
    marks = jnp.broadcast_to(jnp.where(marks_ref[...] == 1, 1.0, 0.0), (tok, tok)).astype(BF)
    return nt(lower, marks), nt(marks, lower), row, col


def identity(size):
    row = lax.broadcasted_iota(jnp.int32, (size, size), 0)
    col = lax.broadcasted_iota(jnp.int32, (size, size), 1)
    return jnp.where(row == col, 1.0, 0.0).astype(BF)


def reversal():
    row = lax.broadcasted_iota(jnp.int32, (TILE, TILE), 0)
    col = lax.broadcasted_iota(jnp.int32, (TILE, TILE), 1)
    return jnp.where(row + col == TILE - 1, 1.0, 0.0).astype(BF)


def fill_shifts(shift_ref, marks_ref, short, forward):
    seg_col, seg_row, row, col = segments(marks_ref)
    tok = marks_ref.shape[1]
    same = seg_col == seg_row
    for lag in range(short):
        hit = (row - col == lag) if forward else (col - row == lag)
        shift_ref[lag * tok : (lag + 1) * tok, :] = jnp.where(hit & same, 1.0, 0.0).astype(BF)


def feats_kernel(marks, x, w, tails, ups, feats, mixed_t, mixed_tail, gate_head, shifts):
    short = w.shape[1]
    tok = marks.shape[1]

    @pl.when(pl.program_id(0) == 0)
    def _():
        fill_shifts(shifts, marks, short, True)

    seg_col, seg_row, _, _ = segments(marks)
    block = x.shape[1]
    eye = identity(block)
    outs = []
    rows = []
    for j in range(3):
        moved = nt(shifts[...], x[j])
        total = w[j, 0:1, :] * moved[0:tok]
        for lag in range(1, short):
            total = total + w[j, lag : lag + 1, :] * moved[lag * tok : (lag + 1) * tok]
        pad = jnp.concatenate(
            [tails[j].astype(F32), jnp.zeros((EDGE_ROWS, block), F32)], axis=0
        )
        fix = jnp.zeros((EDGE_ROWS, block), F32)
        for lag in range(1, short):
            fix = fix + w[j, lag : lag + 1, :] * pad[EDGE_ROWS - lag : 2 * EDGE_ROWS - lag]
        head = total[0:EDGE_ROWS] + jnp.where(seg_col[0:EDGE_ROWS, 0:block] == 0, fix, 0.0)
        total = jnp.concatenate([head, total[EDGE_ROWS:]], axis=0).astype(BF)
        rows.append(total)
        outs.append(nt(eye, total))
        feats[j] = outs[j].astype(BF)
    product = (rows[1].astype(F32) * rows[2].astype(F32)).astype(BF)
    flip = reversal()
    for b in range(tok // TILE):
        span = slice(b * TILE, (b + 1) * TILE)
        mixed_t[span, :] = nn(flip, product[span]).astype(BF)
    mixed = outs[1][:, tok - TILE :] * outs[2][:, tok - TILE :]
    first = seg_row[0:1, :]
    open_end = first[:, tok - TILE :] == first[:, tok - 1 : tok]
    mixed_tail[...] = jnp.where(open_end, mixed, 0.0).astype(BF)
    gate = ups[...].astype(F32) * outs[0][:, 0:TILE]
    gate_head[...] = jnp.where(first[:, 0:TILE] == 0, gate, 0.0).astype(BF)


def circulant(filt, g):
    row = filt[g : g + 1, :].astype(BF).astype(F32)
    wide = jnp.broadcast_to(row, (TILE, TILE))
    return pltpu.roll(wide, 0, 1, stride=1, stride_axis=0).astype(BF)


def diagonals(product):
    moved = pltpu.roll(product, 1, 1, stride=1, stride_axis=0)
    return jnp.sum(moved, axis=0, keepdims=True)


def own_kernel(members, marks, feats, ups, mixed_t, filt, conv, back, part):
    seg_col, seg_row, row, col = segments(marks)
    block = feats.shape[1]
    masks = []
    masks_bf = []
    for b in range(2):
        lo = b * TILE
        span = slice(lo, lo + TILE)
        keep = (seg_col[span, span] == seg_row[span, span]) & (col[span, span] >= row[span, span])
        masks_bf.append(jnp.where(keep, 1.0, 0.0).astype(BF))
        masks.append(nn(reversal(), masks_bf[b]))
    mixed = (feats[1].astype(F32) * feats[2].astype(F32)).astype(BF)
    gate = (ups[...].astype(F32) * feats[0].astype(F32)).astype(BF)
    lane = lax.broadcasted_iota(jnp.int32, (TILE, TILE), 1)
    for g in range(block // members):
        table = circulant(filt, g)
        rows = slice(g * members, (g + 1) * members)
        cb = (g * members) // TILE
        mine = (lane >= g * members - cb * TILE) & (lane < (g + 1) * members - cb * TILE)
        mine_bf = jnp.where(mine, 1.0, 0.0).astype(BF)
        total = None
        for b in range(2):
            span = slice(b * TILE, (b + 1) * TILE)
            diag = table * masks_bf[b]
            conv[rows, span] = nn(mixed[rows, span], diag)
            back[rows, span] = nt(gate[rows, span], diag)
            chans = slice(cb * TILE, (cb + 1) * TILE)
            product = nn(mixed_t[span, chans] * mine_bf, gate[chans, span]) * masks[b]
            total = product if total is None else total + product
        part[g : g + 1, :] = diagonals(total)


def grads_kernel(
    members, marks, x, w, tails, feats, ups, mixed_t, mixed_halo, gate_halo, conv, back, filt, part,
    mixed_out, grads, heads, short_grad, filt_grad, shifts, conv_s, back_s,
):
    short = w.shape[1]
    tok = marks.shape[1]
    block = x.shape[1]

    @pl.when(pl.program_id(0) == 0)
    def _():
        fill_shifts(shifts, marks, short, False)

    seg_col, seg_row, row, col = segments(marks)
    eye = identity(block)
    first = seg_row[0:1, :]
    middle = first[:, TILE - 1 : TILE]
    last = first[:, tok - 1 : tok]
    from_start = [
        jnp.where(first[:, 0:TILE] == 0, 1.0, 0.0),
        jnp.where(first[:, TILE:] == middle, 1.0, 0.0),
    ]
    to_end = [
        jnp.where(first[:, 0:TILE] == middle, 1.0, 0.0),
        jnp.where(first[:, TILE:] == last, 1.0, 0.0),
    ]
    upper_bf = jnp.where(col[0:TILE, 0:TILE] < row[0:TILE, 0:TILE], 1.0, 0.0).astype(BF)
    upper = jnp.where(col[0:TILE, 0:TILE] + row[0:TILE, 0:TILE] < TILE - 1, 1.0, 0.0)
    fq = feats[0].astype(F32)
    fk = feats[1].astype(F32)
    fv = feats[2].astype(F32)
    up = ups[...].astype(F32)
    mixed0 = ((fk[:, 0:TILE] * fv[:, 0:TILE]) * to_end[0]).astype(BF)
    gate1 = ((up[:, TILE:] * fq[:, TILE:]) * from_start[1]).astype(BF)
    mixed_h = mixed_halo[...]
    gate_h = gate_halo[...]
    gate0 = ((up[:, 0:TILE] * fq[:, 0:TILE]) * from_start[0]).astype(BF)
    mixed_ht = nt(reversal(), mixed_h).astype(BF)
    keep_col = (seg_col[0:TILE, 0:TILE] == seg_col[TILE - 1 : TILE, 0:TILE])
    keep_bf = nn(reversal(), jnp.where(keep_col, 1.0, 0.0).astype(BF)).astype(BF)
    lane = lax.broadcasted_iota(jnp.int32, (TILE, TILE), 1)
    for g in range(block // members):
        table = circulant(filt, g) * upper_bf
        rows = slice(g * members, (g + 1) * members)
        cb = (g * members) // TILE
        chans = slice(cb * TILE, (cb + 1) * TILE)
        mine = (lane >= g * members - cb * TILE) & (lane < (g + 1) * members - cb * TILE)
        mine_bf = jnp.where(mine, 1.0, 0.0).astype(BF)
        ahead = nn(jnp.concatenate([mixed_h[rows], mixed0[rows]], axis=0), table)
        conv_s[rows, 0:TILE] = conv[rows, 0:TILE] + ahead[0:members] * from_start[0]
        conv_s[rows, TILE:] = conv[rows, TILE:] + ahead[members:] * from_start[1]
        behind = nt(jnp.concatenate([gate1[rows], gate_h[rows]], axis=0), table)
        back_s[rows, 0:TILE] = back[rows, 0:TILE] + behind[0:members] * to_end[0]
        back_s[rows, TILE:] = back[rows, TILE:] + behind[members:] * to_end[1]
        product = nn(mixed_ht[:, chans] * mine_bf, gate0[chans]) + nn(
            mixed_t[0:TILE, chans] * (keep_bf * mine_bf), gate1[chans]
        )
        filt_grad[g : g + 1, :] = part[g : g + 1, :] + diagonals(product * upper)
    conv_v = conv_s[...]
    back_v = back_s[...]
    mixed_out[...] = (fq * conv_v).astype(BF)
    feat_grad = [
        (up * conv_v).astype(BF),
        (back_v * fv).astype(BF),
        (back_v * fk).astype(BF),
    ]
    open_start = seg_col[0:EDGE_ROWS, 0:block] == 0
    for j in range(3):
        moved = nt(shifts[...], feat_grad[j])
        raw = nt(eye, x[j])
        head = jnp.where(open_start, moved[0:EDGE_ROWS], 0.0)
        heads[j] = head.astype(BF)
        pad = jnp.concatenate(
            [tails[j].astype(F32), jnp.zeros((EDGE_ROWS, block), F32)], axis=0
        )
        total = None
        sums = []
        for lag in range(short):
            piece = moved[lag * tok : (lag + 1) * tok]
            term = w[j, lag : lag + 1, :] * piece
            total = term if total is None else total + term
            column = jnp.sum(raw * piece, axis=0, keepdims=True)
            if lag > 0:
                cross = head * pad[EDGE_ROWS - lag : 2 * EDGE_ROWS - lag]
                column = column + jnp.sum(cross, axis=0, keepdims=True)
            sums.append(column)
        sums.append(jnp.zeros((1, block), F32))
        stacked = jnp.concatenate(sums, axis=0)
        for h in range(block // TILE):
            short_grad[j, h] = stacked[:, h * TILE : (h + 1) * TILE]
        grads[j] = nt(eye, total.astype(BF)).astype(BF)


def fix_kernel(marks, w, next_heads, grads_in, grads):
    short = w.shape[1]
    tok = marks.shape[1]
    block = grads.shape[1]
    seg_col, _, _, _ = segments(marks)
    open_end = seg_col[tok - EDGE_ROWS :, 0:block] == seg_col[tok - 1 : tok, 0:block]
    eye = identity(block)
    for j in range(3):
        pad = jnp.concatenate(
            [jnp.zeros((EDGE_ROWS, block), F32), next_heads[j].astype(F32)], axis=0
        )
        fix = jnp.zeros((EDGE_ROWS, block), F32)
        for lag in range(1, short):
            fix = fix + w[j, lag : lag + 1, :] * pad[lag : lag + EDGE_ROWS]
        fix = jnp.where(open_end, fix, 0.0)
        wide = jnp.concatenate([jnp.zeros((TILE - EDGE_ROWS, block), F32), fix], axis=0)
        grads[j] = (grads_in[j].astype(F32) + nt(eye, wide.astype(BF))).astype(BF)


def shapes(*items):
    return [jax.ShapeDtypeStruct(s, d) for s, d in items]


def params():
    return pltpu.CompilerParams(vmem_limit_bytes=LIMIT)


def step_forward(block, size):
    return lax.ppermute(block, SEQ, [(i, i + 1) for i in range(size - 1)])


def step_back(block, size):
    return lax.ppermute(block, SEQ, [(i + 1, i) for i in range(size - 1)])


def exchange(pieces, axes):
    return lax.all_to_all(pieces, axes, 0, 0)


def local(streams, short_taps, long_taps, doc_marks, upstream):
    chan, tok = streams.shape[1:]
    groups, taps = long_taps.shape
    short = short_taps.shape[2]
    members = chan // groups
    steps = chan // BLOCK
    per = BLOCK // members
    size = lax.axis_size(SEQ)
    w = jnp.transpose(short_taps, (0, 2, 1))
    marks = doc_marks.reshape(1, tok)

    late = doc_marks[tok - EDGE_ROWS :]
    spots = jnp.arange(EDGE_ROWS)
    blocked = jnp.sum(jnp.where(spots[None, :] > spots[:, None], late[None, :], 0), axis=1)
    open_tail = (blocked == 0).astype(BF)
    tails = step_forward(
        jnp.transpose(streams[:, :, tok - EDGE_ROWS :] * open_tail, (0, 2, 1)), size
    )

    one = pl.BlockSpec((1, tok), lambda i: (0, 0))
    three = pl.BlockSpec((3, BLOCK, tok), lambda i: (0, i, 0))
    wspec = pl.BlockSpec((3, short, BLOCK), lambda i: (0, 0, i))
    espec = pl.BlockSpec((3, EDGE_ROWS, BLOCK), lambda i: (0, 0, i))
    full = pl.BlockSpec((BLOCK, tok), lambda i: (i, 0))
    tile0 = pl.BlockSpec((BLOCK, TILE), lambda i: (i, 0))
    tspec = pl.BlockSpec((tok, BLOCK), lambda i: (0, i))
    fspec = pl.BlockSpec((per, taps), lambda i: (i, 0))

    feats, mixed_t, mixed_tail, gate_head = pl.pallas_call(
        feats_kernel,
        grid=(steps,),
        in_specs=[one, three, wspec, espec, tile0],
        out_specs=[three, tspec, tile0, tile0],
        out_shape=shapes(
            ((3, chan, tok), BF), ((tok, chan), BF), ((chan, TILE), BF), ((chan, TILE), BF)
        ),
        scratch_shapes=[pltpu.VMEM((short * tok, tok), BF)],
        compiler_params=params(),
    )(marks, streams, w, tails, upstream)
    mixed_halo = step_forward(mixed_tail, size)
    gate_halo = step_back(gate_head, size)

    conv, back, part = pl.pallas_call(
        functools.partial(own_kernel, members),
        grid=(steps,),
        in_specs=[one, three, full, tspec, fspec],
        out_specs=[full, full, fspec],
        out_shape=shapes(((chan, tok), F32), ((chan, tok), F32), ((groups, taps), F32)),
        compiler_params=params(),
        cost_estimate=pl.CostEstimate(flops=2 * 10**9, bytes_accessed=8 * 10**6, transcendentals=0),
    )(marks, feats, upstream, mixed_t, long_taps)

    mixed_out, grads, heads, short_part, filt_part = pl.pallas_call(
        functools.partial(grads_kernel, members),
        grid=(steps,),
        in_specs=[
            one, three, wspec, espec, three, full, tspec, tile0, tile0, full, full, fspec, fspec
        ],
        out_specs=[
            full, three, espec,
            pl.BlockSpec((3, BLOCK // TILE, EDGE_ROWS, TILE), lambda i: (0, i, 0, 0)),
            fspec,
        ],
        out_shape=shapes(
            ((chan, tok), BF), ((3, chan, tok), BF), ((3, EDGE_ROWS, chan), BF),
            ((3, chan // TILE, EDGE_ROWS, TILE), F32), ((groups, taps), F32),
        ),
        scratch_shapes=[
            pltpu.VMEM((short * tok, tok), BF),
            pltpu.VMEM((BLOCK, tok), F32),
            pltpu.VMEM((BLOCK, tok), F32),
        ],
        compiler_params=params(),
    )(
        marks, streams, w, tails, feats, upstream, mixed_t, mixed_halo, gate_halo, conv, back,
        long_taps, part,
    )
    next_heads = step_back(heads, size)

    cube = lax.axis_size(CUBE)
    rest = lax.axis_size("zh")
    tp = lax.axis_size(TP)
    flat = jnp.concatenate([filt_part, short_part.reshape(-1, TILE)], axis=0)
    share = flat.shape[0] // cube
    mine = jnp.sum(exchange(flat.reshape(cube, share, TILE), CUBE), axis=0)
    mine = jnp.sum(exchange(jnp.broadcast_to(mine, (rest,) + mine.shape), "zh"), axis=0)
    total = exchange(jnp.broadcast_to(mine, (cube,) + mine.shape), CUBE).reshape(flat.shape)
    square = jnp.sum(total * total)
    squares = exchange(jnp.broadcast_to(square, (tp, EDGE_ROWS, TILE)), TP)
    entries = tp * (groups * taps + 3 * chan * short)
    mean = jnp.sum(squares[:, 0, 0]) / entries
    scale = jnp.minimum(1.0, 1.0 / jnp.sqrt(mean + 1e-06))

    last = pl.BlockSpec((3, BLOCK, TILE), lambda i: (0, i, tok // TILE - 1))
    grads = pl.pallas_call(
        fix_kernel,
        grid=(steps,),
        in_specs=[one, wspec, espec, last],
        out_specs=last,
        out_shape=jax.ShapeDtypeStruct(grads.shape, BF),
        input_output_aliases={3: 0},
        compiler_params=params(),
    )(marks, w, next_heads, grads)
    total = total * scale
    grad_long = total[0:groups]
    grad_short = total[groups:].reshape(3, chan // TILE, EDGE_ROWS, TILE)[:, :, 0:short]
    grad_short = jnp.transpose(grad_short, (0, 1, 3, 2)).reshape(3, chan, short)
    return (mixed_out, grads, grad_long, grad_short)


def solution(mesh):
    fine = Mesh(mesh.devices.reshape(4, 4, 4, 4, 2), ("x", "zh", "zl", "y", "c"))
    in_specs = (P(None, TP, SEQ), P(None, TP, None), P(TP, None), P(SEQ), P(TP, SEQ))
    out_specs = (P(TP, SEQ), P(None, TP, SEQ), P(TP, None), P(None, TP, None))
    return jax.shard_map(local, mesh=fine, in_specs=in_specs, out_specs=out_specs, check_vma=False)
```

```python
import functools

import jax
import jax.numpy as jnp
from jax import lax
from jax.experimental import pallas as pl
from jax.experimental.pallas import tpu as pltpu
from jax.sharding import Mesh
from jax.sharding import PartitionSpec as P

BF = jnp.bfloat16
F32 = jnp.float32
SEQ = ("x", "zh", "zl")
TP = ("y", "c")
CUBE = ("x", "zl")
TILE = 128
EDGE = 8
PACK = 16
BLOCK = 256
LIMIT = 24 * 1024 * 1024
FIRST_LIMIT = 57 * 1024 * 1024


def nt(left, right):
    return lax.dot_general(left, right, (((1,), (1,)), ((), ())), preferred_element_type=F32)


def nn(left, right):
    return lax.dot_general(left, right, (((1,), (0,)), ((), ())), preferred_element_type=F32)


def ones_where(keep):
    return jnp.where(keep, 1.0, 0.0).astype(BF)


def grid_of(rows, cols):
    return (
        lax.broadcasted_iota(jnp.int32, (rows, cols), 0),
        lax.broadcasted_iota(jnp.int32, (rows, cols), 1),
    )


def segments(marks):
    tok = marks.shape[1]
    row, col = grid_of(tok, tok)
    lower = ones_where(col <= row)
    wide = jnp.broadcast_to(jnp.where(marks[...] == 1, 1.0, 0.0), (tok, tok)).astype(BF)
    return nt(lower, wide), nt(wide, lower), row, col


def identity(size):
    row, col = grid_of(size, size)
    return ones_where(row == col)


def reversal():
    row, col = grid_of(TILE, TILE)
    return ones_where(row + col == TILE - 1)


def fill_shifts(shifts, same, offset, short):
    tok = same.shape[0]
    for lag in range(short):
        shifts[lag * tok : (lag + 1) * tok, :] = ones_where((offset == lag) & same)


def tap_columns(w, j, span):
    short = w.shape[1]
    wide = jnp.concatenate(
        [w[j, :, span], jnp.zeros((EDGE - short, BLOCK), F32)], axis=0
    )
    return jnp.transpose(wide)


def weighted(values, taps, short):
    parts = []
    values = values.astype(F32)
    for lag in range(short):
        tap = jnp.broadcast_to(taps[:, lag : lag + 1], (BLOCK, TILE))
        for lo in range(0, values.shape[1], TILE):
            parts.append((values[:, lo : lo + TILE] * tap).astype(BF))
    return jnp.concatenate(parts, axis=1)


def edge_rows(packed, first, j, lo):
    rows = []
    for tile in range(lo // TILE, (lo + BLOCK) // TILE):
        at = first + (2 * tile + j // 2) * PACK
        rows.append(packed[at : at + PACK, :].astype(F32)[(j % 2) * EDGE : (j % 2 + 1) * EDGE])
    return jnp.concatenate(rows, axis=1)


def border_sum(w, j, span, pad, forward):
    total = None
    for lag in range(1, w.shape[1]):
        lo = EDGE - lag if forward else lag
        term = w[j, lag : lag + 1, span] * pad[lo : lo + EDGE]
        total = term if total is None else total + term
    return total


def after(rows):
    return jnp.concatenate([rows, jnp.zeros_like(rows)], axis=0)


def at_front(rows, eye):
    wide = jnp.concatenate([rows, jnp.zeros((TILE - EDGE, rows.shape[1]), F32)], axis=0)
    return nt(eye, wide.astype(BF))


def feats_kernel(marks, x, w, ups, feats, next_pack, last_pack, shifts):
    short = w.shape[1]
    chan, tok = ups.shape
    seg_col, seg_row, row, col = segments(marks)
    fill_shifts(shifts, seg_col == seg_row, col - row, short)
    first = seg_row[0:1, :]
    open_end = first == first[:, tok - 1 : tok]
    open_start = first == 0
    head_row, head_col = grid_of(PACK, tok)
    take_tail = ones_where((head_col == tok - EDGE + head_row) & open_end & (head_row < EDGE))
    take_head = ones_where((head_col == head_row) & (head_row < EDGE) & open_start)
    for lo in range(0, chan, BLOCK):
        span = slice(lo, lo + BLOCK)
        outs = []
        tails = []
        for j in range(3):
            raw = x[j, span]
            taps = tap_columns(w, j, span)
            out = nn(weighted(raw, taps, short), shifts[...]).astype(BF)
            feats[j, span] = out
            outs.append(out.astype(F32))
            tails.append(nt(take_tail, raw)[0:EDGE])
        tails.append(jnp.zeros_like(tails[0]))
        mixed = outs[1][:, tok - TILE :] * outs[2][:, tok - TILE :]
        next_pack[span, :] = jnp.where(open_end[:, tok - TILE :], mixed, 0.0).astype(BF)
        up = ups[span]
        gate = up[:, 0:TILE].astype(F32) * outs[0][:, 0:TILE]
        last_pack[span, :] = jnp.where(open_start[:, 0:TILE], gate, 0.0).astype(BF)
        heads = nt(take_head, up).astype(BF)
        pairs = [
            jnp.concatenate([tails[p], tails[p + 1]], axis=0).astype(BF) for p in (0, 2)
        ]
        for h in range(0, BLOCK, TILE):
            tile = (lo + h) // TILE
            at = chan + tile * PACK
            last_pack[at : at + PACK, :] = heads[:, h : h + TILE]
            for p in range(2):
                at = chan + (2 * tile + p) * PACK
                next_pack[at : at + PACK, :] = pairs[p][:, h : h + TILE]


def circulant(filt, g):
    row = filt[g : g + 1, :].astype(BF).astype(F32)
    wide = jnp.broadcast_to(row, (TILE, TILE))
    return pltpu.roll(wide, 0, 1, stride=1, stride_axis=0).astype(BF)


def diagonals(product):
    moved = pltpu.roll(product, 1, 1, stride=1, stride_axis=0)
    return jnp.sum(moved, axis=0, keepdims=True)


def members_mask(start, members):
    row, col = grid_of(TILE, TILE)
    return ones_where((col >= start) & (col < start + members))


def own_kernel(members, marks, feats, ups, filt, conv, back, part):
    chan, tok = ups.shape
    seg_col, seg_row, row, col = segments(marks)
    flip = reversal()
    s = slice(TILE, tok)
    keep_bf = ones_where((seg_col[s, s] == seg_row[s, s]) & (col[s, s] >= row[s, s]))
    keep = nn(flip, keep_bf)
    picks = [members_mask(p, members) for p in range(0, TILE, members)]
    for lo in range(0, chan, BLOCK):
        span = slice(lo, lo + BLOCK)
        mixed = (feats[1, span, s].astype(F32) * feats[2, span, s].astype(F32)).astype(BF)
        gate = (ups[span, s].astype(F32) * feats[0, span, s].astype(F32)).astype(BF)
        mixed_t = nt(flip, mixed).astype(BF)
        for g in range(BLOCK // members):
            n = lo // members + g
            table = circulant(filt, n) * keep_bf
            rows = slice(g * members, (g + 1) * members)
            at = slice(lo + g * members, lo + (g + 1) * members)
            cb = (g * members) // TILE
            chans = slice(cb * TILE, (cb + 1) * TILE)
            conv[at, :] = nn(mixed[rows], table)
            back[at, :] = nt(gate[rows], table)
            product = nn(mixed_t[:, chans] * picks[g % len(picks)], gate[chans])
            part[n : n + 1, :] = diagonals(product * keep)


def halo_kernel(
    members, marks, x, w, feats, ups, from_last, from_next, conv, back, filt, part, shifts,
    mixed_out, grads, heads, sums, conv_s, back_s,
):
    short = w.shape[1]
    chan, tok = ups.shape
    seg_col, seg_row, row, col = segments(marks)
    eye = identity(BLOCK)
    flip = reversal()
    first = seg_row[0:1, :]
    middle = first[:, TILE - 1 : TILE]
    last = first[:, tok - 1 : tok]
    from_start = [
        jnp.where(first[:, 0:TILE] == 0, 1.0, 0.0),
        jnp.where(first[:, TILE:] == middle, 1.0, 0.0),
    ]
    to_end = [
        jnp.where(first[:, 0:TILE] == middle, 1.0, 0.0),
        jnp.where(first[:, TILE:] == last, 1.0, 0.0),
    ]
    row_t, col_t = grid_of(TILE, TILE)
    upper_bf = ones_where(col_t < row_t)
    upper = jnp.where(col_t + row_t < TILE - 1, 1.0, 0.0)
    s = slice(0, TILE)
    keep_bf = ones_where((seg_col[s, s] == seg_row[s, s]) & (col[s, s] >= row[s, s]))
    keep = nn(flip, keep_bf)
    open_start = seg_col[0:EDGE, 0:BLOCK] == 0
    head_row, head_col = grid_of(EDGE, tok)
    take_head = ones_where((head_col == head_row) & (first == 0))
    take_tail = ones_where((head_col == tok - EDGE + head_row) & (first == last))
    picks = [members_mask(p, members) for p in range(0, TILE, members)]
    per = BLOCK // members
    stride = per + 3 * (BLOCK // TILE) * EDGE
    for lo in range(0, chan, BLOCK):
        span = slice(lo, lo + BLOCK)
        pads = [after(edge_rows(from_last, chan, j, lo)) for j in range(3)]
        feat = []
        for j in range(3):
            fix = jnp.where(open_start, border_sum(w, j, span, pads[j], True), 0.0)
            head = (feats[j, span, 0:TILE].astype(F32) + at_front(fix, eye)).astype(BF)
            feat.append(jnp.concatenate([head, feats[j, span, TILE:]], axis=1).astype(F32))
        up = ups[span].astype(F32)
        gate = up * feat[0]
        mixed = feat[1][:, 0:TILE] * feat[2][:, 0:TILE]
        mixed_b = mixed.astype(BF)
        gate_b = gate[:, 0:TILE].astype(BF)
        mixed0 = (mixed * to_end[0]).astype(BF)
        gate0 = (gate[:, 0:TILE] * from_start[0]).astype(BF)
        gate1 = (gate[:, TILE:] * from_start[1]).astype(BF)
        mixed_h = from_last[span]
        beyond = border_sum(w, 0, span, after(nt(take_tail, x[0, span])), True)
        ups_head = jnp.concatenate(
            [
                from_next[at : at + PACK, :].astype(F32)[0:EDGE]
                for at in range(chan + lo // TILE * PACK, chan + (lo + BLOCK) // TILE * PACK, PACK)
            ],
            axis=1,
        )
        gate_h = (from_next[span].astype(F32) + at_front(ups_head * beyond, eye)).astype(BF)
        lead_t = nt(flip, mixed_h).astype(BF)
        mixed_t = nt(flip, mixed0).astype(BF)
        whole_t = nt(flip, mixed_b).astype(BF)
        base = lo // BLOCK * stride
        for g in range(per):
            n = lo // members + g
            table = circulant(filt, n)
            diag = table * keep_bf
            table = table * upper_bf
            rows = slice(g * members, (g + 1) * members)
            at = slice(lo + g * members, lo + (g + 1) * members)
            cb = (g * members) // TILE
            chans = slice(cb * TILE, (cb + 1) * TILE)
            pick = picks[g % len(picks)]
            ahead = nn(jnp.concatenate([mixed_h[rows], mixed0[rows]], axis=0), table)
            conv_s[rows, 0:TILE] = nn(mixed_b[rows], diag) + ahead[0:members] * from_start[0]
            conv_s[rows, TILE:] = conv[at] + ahead[members:] * from_start[1]
            behind = nt(jnp.concatenate([gate1[rows], gate_h[rows]], axis=0), table)
            back_s[rows, 0:TILE] = nt(gate_b[rows], diag) + behind[0:members] * to_end[0]
            back_s[rows, TILE:] = back[at] + behind[members:] * to_end[1]
            product = nn(lead_t[:, chans] * pick, gate0[chans]) + nn(
                mixed_t[:, chans] * pick, gate1[chans]
            )
            inner = nn(whole_t[:, chans] * pick, gate_b[chans])
            sums[base + g : base + g + 1, :] = part[n : n + 1, :] + diagonals(
                product * upper + inner * keep
            )
        conv_v = conv_s[...]
        back_v = back_s[...]
        mixed_out[span, :] = (feat[0] * conv_v).astype(BF)
        grad = [
            (up * conv_v).astype(BF),
            (back_v * feat[2]).astype(BF),
            (back_v * feat[1]).astype(BF),
        ]
        for j in range(3):
            grads[j, span] = grad[j]
            moved = nt(shifts[...], grad[j])
            raw = nt(eye, x[j, span])
            head = nt(take_head, grad[j])
            heads[j, :, span] = head.astype(BF)
            columns = []
            for lag in range(short):
                piece = moved[lag * tok : (lag + 1) * tok]
                column = jnp.sum(raw * piece, axis=0, keepdims=True)
                if lag > 0:
                    cross = head * pads[j][EDGE - lag : 2 * EDGE - lag]
                    column = column + jnp.sum(cross, axis=0, keepdims=True)
                columns.append(column)
            columns += [jnp.zeros((1, BLOCK), F32)] * (EDGE - short)
            stacked = jnp.concatenate(columns, axis=0)
            for h in range(BLOCK // TILE):
                at = base + per + (j * (BLOCK // TILE) + h) * EDGE
                sums[at : at + EDGE, :] = stacked[:, h * TILE : (h + 1) * TILE]


def streams_kernel(marks, w, grads, next_heads, out, shifts):
    short = w.shape[1]
    tok = marks.shape[1]
    seg_col, seg_row, row, col = segments(marks)
    fill_shifts(shifts, seg_col == seg_row, row - col, short)
    open_end = seg_col[tok - EDGE :, 0:BLOCK] == seg_col[tok - 1 : tok, 0:BLOCK]
    eye = identity(BLOCK)
    for lo in range(0, grads.shape[1], BLOCK):
        span = slice(lo, lo + BLOCK)
        for j in range(3):
            taps = tap_columns(w, j, span)
            total = nn(weighted(grads[j, span], taps, short), shifts[...])
            pad = next_heads[j, :, span].astype(F32)
            pad = jnp.concatenate([jnp.zeros_like(pad), pad], axis=0)
            fix = jnp.where(open_end, border_sum(w, j, span, pad, False), 0.0)
            wide = jnp.concatenate([jnp.zeros((TILE - EDGE, BLOCK), F32), fix], axis=0)
            out[j, span, 0:TILE] = total[:, 0:TILE].astype(BF)
            out[j, span, TILE:] = (total[:, TILE:] + nt(eye, wide.astype(BF))).astype(BF)


def squares_kernel(total, out):
    value = total[...]
    out[...] = jnp.broadcast_to(jnp.sum(value * value), out.shape)


def scale_kernel(entries, total, squares, grad_long, grad_short):
    mean = jnp.sum(squares[:, 0, 0:1]) / entries
    wide = jnp.broadcast_to(mean, (EDGE, TILE))
    scale = jnp.minimum(1.0, 1.0 / jnp.sqrt(wide + 1e-06))[0:1]
    short = grad_short.shape[1]
    members = grad_short.shape[2] // grad_long.shape[0]
    per = BLOCK // members
    stride = per + 3 * (BLOCK // TILE) * EDGE
    for b in range(grad_short.shape[2] // BLOCK):
        base = b * stride
        grad_long[b * per : (b + 1) * per, :] = total[base : base + per, :] * scale
        for j in range(3):
            for h in range(BLOCK // TILE):
                at = base + per + (j * (BLOCK // TILE) + h) * EDGE
                lane = b * BLOCK + h * TILE
                grad_short[j, :, lane : lane + TILE] = total[at : at + short, :] * scale


def call(kernel, outs, scratch, *args, limit=LIMIT):
    return pl.pallas_call(
        kernel,
        in_specs=[pl.BlockSpec(memory_space=pltpu.VMEM) for _ in args],
        out_specs=[pl.BlockSpec(memory_space=pltpu.VMEM) for _ in outs],
        out_shape=[jax.ShapeDtypeStruct(s, d) for s, d in outs],
        scratch_shapes=scratch,
        compiler_params=pltpu.CompilerParams(vmem_limit_bytes=limit),
        cost_estimate=pl.CostEstimate(
            flops=2 * 10**9, bytes_accessed=8 * 10**6, transcendentals=0
        ),
    )(*args)


def step_forward(block, size):
    return lax.ppermute(block, SEQ, [(i, i + 1) for i in range(size - 1)])


def step_back(block, size):
    return lax.ppermute(block, SEQ, [(i + 1, i) for i in range(size - 1)])


def exchange(pieces, axes):
    return lax.all_to_all(pieces, axes, 0, 0)


def local(streams, short_taps, long_taps, doc_marks, upstream):
    chan, tok = streams.shape[1:]
    groups, taps = long_taps.shape
    short = short_taps.shape[2]
    members = chan // groups
    size = lax.axis_size(SEQ)
    w = jnp.transpose(short_taps, (0, 2, 1))
    marks = doc_marks.reshape(1, tok)
    shifts = ((short * tok, tok), BF)
    whole = ((3, chan, tok), BF)
    tiles = chan // TILE

    feats, next_pack, last_pack, moves = call(
        feats_kernel,
        [
            whole, ((chan + 2 * tiles * PACK, TILE), BF), ((chan + tiles * PACK, TILE), BF),
            shifts,
        ],
        [],
        marks, streams, w, upstream,
        limit=FIRST_LIMIT,
    )
    from_last = step_forward(next_pack, size)
    from_next = step_back(last_pack, size)

    half = ((chan, TILE), F32)
    conv, back, part = call(
        functools.partial(own_kernel, members),
        [half, half, ((groups, taps), F32)],
        [],
        marks, feats, upstream, long_taps,
    )
    rows = groups + 3 * tiles * EDGE
    mixed_out, feat_grad, heads, sums = call(
        functools.partial(halo_kernel, members),
        [((chan, tok), BF), whole, ((3, EDGE, chan), BF), ((rows, TILE), F32)],
        [pltpu.VMEM((BLOCK, tok), F32), pltpu.VMEM((BLOCK, tok), F32)],
        marks, streams, w, feats, upstream, from_last, from_next, conv, back, long_taps, part, moves,
    )
    next_heads = step_back(heads, size)

    cube = lax.axis_size(CUBE)
    rest = lax.axis_size("zh")
    tp = lax.axis_size(TP)
    mine = jnp.sum(exchange(sums.reshape(cube, rows // cube, TILE), CUBE), axis=0)
    mine, feat_grad, next_heads = lax.optimization_barrier((mine, feat_grad, next_heads))
    mine = jnp.sum(exchange(jnp.broadcast_to(mine, (rest,) + mine.shape), "zh"), axis=0)
    (grad_streams,) = call(
        streams_kernel, [whole], [pltpu.VMEM(*shifts)], marks, w, feat_grad, next_heads
    )
    mine, grad_streams = lax.optimization_barrier((mine, grad_streams))
    total = exchange(jnp.broadcast_to(mine, (cube,) + mine.shape), CUBE).reshape(rows, TILE)
    (squares,) = call(squares_kernel, [((tp, EDGE, TILE), F32)], [], total)
    squares = exchange(squares, TP)
    entries = tp * (groups * taps + 3 * chan * short)
    grad_long, grad_short = call(
        functools.partial(scale_kernel, entries),
        [((groups, taps), F32), ((3, short, chan), F32)],
        [],
        total, squares,
    )
    return (mixed_out, grad_streams, grad_long, jnp.transpose(grad_short, (0, 2, 1)))


def solution(mesh):
    fine = Mesh(mesh.devices.reshape(4, 4, 4, 4, 2), ("x", "zh", "zl", "y", "c"))
    in_specs = (P(None, TP, SEQ), P(None, TP, None), P(TP, None), P(SEQ), P(TP, SEQ))
    out_specs = (P(TP, SEQ), P(None, TP, SEQ), P(TP, None), P(None, TP, None))
    return jax.shard_map(local, mesh=fine, in_specs=in_specs, out_specs=out_specs, check_vma=False)
```

```python
import functools

import jax
import jax.numpy as jnp
from jax import lax
from jax.experimental import pallas as pl
from jax.experimental.pallas import tpu as pltpu
from jax.sharding import Mesh
from jax.sharding import PartitionSpec as P

BF = jnp.bfloat16
F32 = jnp.float32
SEQ = ("x", "zh", "zl")
TP = ("y", "c")
CUBE = ("x", "zl")
FAR = ("zh", "y", "c")
TILE = 128
EDGE = 8
PACK = 16
BLOCK = 256
LIMIT = 24 * 1024 * 1024
FIRST_LIMIT = 53 * 1024 * 1024


def nt(left, right):
    return lax.dot_general(left, right, (((1,), (1,)), ((), ())), preferred_element_type=F32)


def nn(left, right):
    return lax.dot_general(left, right, (((1,), (0,)), ((), ())), preferred_element_type=F32)


def ones_where(keep):
    return jnp.where(keep, 1.0, 0.0).astype(BF)


def grid_of(rows, cols):
    return (
        lax.broadcasted_iota(jnp.int32, (rows, cols), 0),
        lax.broadcasted_iota(jnp.int32, (rows, cols), 1),
    )


def segments(marks):
    tok = marks.shape[1]
    row, col = grid_of(tok, tok)
    lower = ones_where(col <= row)
    wide = jnp.broadcast_to(jnp.where(marks[...] == 1, 1.0, 0.0), (tok, tok)).astype(BF)
    return nt(lower, wide), nt(wide, lower), row, col


def identity(size):
    row, col = grid_of(size, size)
    return ones_where(row == col)


def reversal():
    row, col = grid_of(TILE, TILE)
    return ones_where(row + col == TILE - 1)


def fill_shifts(shifts, same, offset, short):
    tok = same.shape[0]
    for lag in range(short):
        shifts[lag * tok : (lag + 1) * tok, :] = ones_where((offset == lag) & same)


def tap_columns(w, j, span):
    short = w.shape[1]
    wide = jnp.concatenate(
        [w[j, :, span], jnp.zeros((EDGE - short, BLOCK), F32)], axis=0
    )
    return jnp.transpose(wide)


def weighted(values, taps, short):
    parts = []
    values = values.astype(F32)
    for lag in range(short):
        tap = jnp.broadcast_to(taps[:, lag : lag + 1], (BLOCK, TILE))
        for lo in range(0, values.shape[1], TILE):
            parts.append((values[:, lo : lo + TILE] * tap).astype(BF))
    return jnp.concatenate(parts, axis=1)


def edge_rows(packed, first, j, lo):
    rows = []
    for tile in range(lo // TILE, (lo + BLOCK) // TILE):
        at = first + (2 * tile + j // 2) * PACK
        rows.append(packed[at : at + PACK, :].astype(F32)[(j % 2) * EDGE : (j % 2 + 1) * EDGE])
    return jnp.concatenate(rows, axis=1)


def border_sum(w, j, span, pad, forward):
    total = None
    for lag in range(1, w.shape[1]):
        lo = EDGE - lag if forward else lag
        term = w[j, lag : lag + 1, span] * pad[lo : lo + EDGE]
        total = term if total is None else total + term
    return total


def after(rows):
    return jnp.concatenate([rows, jnp.zeros_like(rows)], axis=0)


def at_front(rows, eye):
    wide = jnp.concatenate([rows, jnp.zeros((TILE - EDGE, rows.shape[1]), F32)], axis=0)
    return nt(eye, wide.astype(BF))


def feats_kernel(marks, x, w, ups, feats, next_pack, last_pack, shifts, mixed_late, gate_late):
    short = w.shape[1]
    chan, tok = ups.shape
    seg_col, seg_row, row, col = segments(marks)
    fill_shifts(shifts, seg_col == seg_row, col - row, short)
    first = seg_row[0:1, :]
    open_end = first == first[:, tok - 1 : tok]
    open_start = first == 0
    head_row, head_col = grid_of(PACK, tok)
    take_tail = ones_where((head_col == tok - EDGE + head_row) & open_end & (head_row < EDGE))
    take_head = ones_where((head_col == head_row) & (head_row < EDGE) & open_start)
    for lo in range(0, chan, BLOCK):
        span = slice(lo, lo + BLOCK)
        outs = []
        tails = []
        for j in range(3):
            raw = x[j, span]
            taps = tap_columns(w, j, span)
            out = nn(weighted(raw, taps, short), shifts[...]).astype(BF)
            feats[j, span] = out
            outs.append(out.astype(F32))
            tails.append(nt(take_tail, raw)[0:EDGE])
        tails.append(jnp.zeros_like(tails[0]))
        mixed = outs[1][:, tok - TILE :] * outs[2][:, tok - TILE :]
        mixed_late[span, :] = mixed.astype(BF)
        next_pack[span, :] = jnp.where(open_end[:, tok - TILE :], mixed, 0.0).astype(BF)
        up = ups[span]
        gate = up.astype(F32) * outs[0]
        gate_late[span, :] = gate[:, tok - TILE :].astype(BF)
        last_pack[span, :] = jnp.where(open_start[:, 0:TILE], gate[:, 0:TILE], 0.0).astype(BF)
        heads = nt(take_head, up).astype(BF)
        pairs = [
            jnp.concatenate([tails[p], tails[p + 1]], axis=0).astype(BF) for p in (0, 2)
        ]
        for h in range(0, BLOCK, TILE):
            tile = (lo + h) // TILE
            at = chan + tile * PACK
            last_pack[at : at + PACK, :] = heads[:, h : h + TILE]
            for p in range(2):
                at = chan + (2 * tile + p) * PACK
                next_pack[at : at + PACK, :] = pairs[p][:, h : h + TILE]


def circulant(filt, g):
    row = filt[g : g + 1, :].astype(BF).astype(F32)
    wide = jnp.broadcast_to(row, (TILE, TILE))
    return pltpu.roll(wide, 0, 1, stride=1, stride_axis=0).astype(BF)


def turned_filters(filt):
    row, col = grid_of(TILE, TILE)
    return nn(filt[...].astype(BF), ones_where((row + col == TILE) | (row + col == 0)))


def spread(block, picks):
    return jnp.concatenate([block * pick for pick in picks], axis=0)


def diagonals(product):
    moved = pltpu.roll(product, 1, 1, stride=1, stride_axis=0)
    return jnp.sum(moved, axis=0, keepdims=True)


def members_mask(start, members):
    row, col = grid_of(TILE, TILE)
    return ones_where((col >= start) & (col < start + members))


def own_kernel(members, marks, mixed_late, gate_late, filt, conv, back, part):
    chan = mixed_late.shape[0]
    tok = marks.shape[1]
    seg_col, seg_row, row, col = segments(marks)
    flip = reversal()
    s = slice(TILE, tok)
    keep_bf = ones_where((seg_col[s, s] == seg_row[s, s]) & (col[s, s] >= row[s, s]))
    keep = nn(flip, keep_bf)
    keep_tbf = ones_where((seg_col[s, s] == seg_row[s, s]) & (col[s, s] <= row[s, s]))
    back_filt = turned_filters(filt)
    picks = [members_mask(p, members) for p in range(0, TILE, members)]
    for lo in range(0, chan, BLOCK):
        span = slice(lo, lo + BLOCK)
        mixed = mixed_late[span]
        gate = gate_late[span]
        mixed_t = nt(flip, mixed).astype(BF)
        for cb in range(BLOCK // TILE):
            chans = slice(cb * TILE, (cb + 1) * TILE)
            products = nn(spread(mixed_t[:, chans], picks), gate[chans])
            for k in range(len(picks)):
                g = cb * len(picks) + k
                n = lo // members + g
                rows = slice(g * members, (g + 1) * members)
                at = slice(lo + g * members, lo + (g + 1) * members)
                conv[at, :] = nn(mixed[rows], circulant(filt, n) * keep_bf)
                back[at, :] = nn(gate[rows], circulant(back_filt, n) * keep_tbf)
                part[n : n + 1, :] = diagonals(products[k * TILE : (k + 1) * TILE] * keep)


def halo_kernel(
    members, marks, x, w, feats, ups, from_last, from_next, conv, back, filt, part, shifts,
    mixed_out, grads, heads, sums, conv_s, back_s,
):
    short = w.shape[1]
    chan, tok = ups.shape
    seg_col, seg_row, row, col = segments(marks)
    eye = identity(BLOCK)
    flip = reversal()
    first = seg_row[0:1, :]
    middle = first[:, TILE - 1 : TILE]
    last = first[:, tok - 1 : tok]
    from_start = [
        jnp.where(first[:, 0:TILE] == 0, 1.0, 0.0),
        jnp.where(first[:, TILE:] == middle, 1.0, 0.0),
    ]
    to_end = [
        jnp.where(first[:, 0:TILE] == middle, 1.0, 0.0),
        jnp.where(first[:, TILE:] == last, 1.0, 0.0),
    ]
    row_t, col_t = grid_of(TILE, TILE)
    upper_bf = ones_where(col_t < row_t)
    upper = jnp.where(col_t + row_t < TILE - 1, 1.0, 0.0)
    s = slice(0, TILE)
    keep_bf = ones_where((seg_col[s, s] == seg_row[s, s]) & (col[s, s] >= row[s, s]))
    keep = nn(flip, keep_bf)
    keep_tbf = ones_where((seg_col[s, s] == seg_row[s, s]) & (col[s, s] <= row[s, s]))
    upper_tbf = ones_where(col_t > row_t)
    back_filt = turned_filters(filt)
    open_start = seg_col[0:EDGE, 0:BLOCK] == 0
    head_row, head_col = grid_of(EDGE, tok)
    take_head = ones_where((head_col == head_row) & (first == 0))
    take_tail = ones_where((head_col == tok - EDGE + head_row) & (first == last))
    picks = [members_mask(p, members) for p in range(0, TILE, members)]
    per = BLOCK // members
    stride = per + 3 * (BLOCK // TILE) * EDGE
    for lo in range(0, chan, BLOCK):
        span = slice(lo, lo + BLOCK)
        pads = [after(edge_rows(from_last, chan, j, lo)) for j in range(3)]
        feat = []
        for j in range(3):
            fix = jnp.where(open_start, border_sum(w, j, span, pads[j], True), 0.0)
            head = (feats[j, span, 0:TILE].astype(F32) + at_front(fix, eye)).astype(BF)
            feat.append(jnp.concatenate([head, feats[j, span, TILE:]], axis=1).astype(F32))
        up = ups[span].astype(F32)
        gate = up * feat[0]
        mixed = feat[1][:, 0:TILE] * feat[2][:, 0:TILE]
        mixed_b = mixed.astype(BF)
        gate_b = gate[:, 0:TILE].astype(BF)
        mixed0 = (mixed * to_end[0]).astype(BF)
        gate0 = (gate[:, 0:TILE] * from_start[0]).astype(BF)
        gate1 = (gate[:, TILE:] * from_start[1]).astype(BF)
        mixed_h = from_last[span]
        beyond = border_sum(w, 0, span, after(nt(take_tail, x[0, span])), True)
        ups_head = jnp.concatenate(
            [
                from_next[at : at + PACK, :].astype(F32)[0:EDGE]
                for at in range(chan + lo // TILE * PACK, chan + (lo + BLOCK) // TILE * PACK, PACK)
            ],
            axis=1,
        )
        gate_h = (from_next[span].astype(F32) + at_front(ups_head * beyond, eye)).astype(BF)
        lead_t = nt(flip, mixed_h).astype(BF)
        mixed_t = nt(flip, mixed0).astype(BF)
        whole_t = nt(flip, mixed_b).astype(BF)
        base = lo // BLOCK * stride
        for cb in range(BLOCK // TILE):
            chans = slice(cb * TILE, (cb + 1) * TILE)
            both = jnp.concatenate(
                [spread(lead_t[:, chans], picks), spread(mixed_t[:, chans], picks)], axis=1
            )
            products = nn(both, jnp.concatenate([gate0[chans], gate1[chans]], axis=0))
            inners = nn(spread(whole_t[:, chans], picks), gate_b[chans])
            for k in range(len(picks)):
                g = cb * len(picks) + k
                n = lo // members + g
                table = circulant(filt, n)
                diag = table * keep_bf
                table = table * upper_bf
                turned = circulant(back_filt, n)
                diag_b = turned * keep_tbf
                turned = turned * upper_tbf
                rows = slice(g * members, (g + 1) * members)
                at = slice(lo + g * members, lo + (g + 1) * members)
                ahead = nn(
                    jnp.concatenate([mixed_h[rows], mixed0[rows], mixed_b[rows]], axis=0),
                    jnp.concatenate([table, diag], axis=1),
                )
                conv_s[rows, 0:TILE] = (
                    ahead[2 * members :, TILE:] + ahead[0:members, 0:TILE] * from_start[0]
                )
                conv_s[rows, TILE:] = (
                    conv[at] + ahead[members : 2 * members, 0:TILE] * from_start[1]
                )
                behind = nn(
                    jnp.concatenate([gate1[rows], gate_h[rows], gate_b[rows]], axis=0),
                    jnp.concatenate([turned, diag_b], axis=1),
                )
                back_s[rows, 0:TILE] = (
                    behind[2 * members :, TILE:] + behind[0:members, 0:TILE] * to_end[0]
                )
                back_s[rows, TILE:] = (
                    back[at] + behind[members : 2 * members, 0:TILE] * to_end[1]
                )
                spots = slice(k * TILE, (k + 1) * TILE)
                sums[base + g : base + g + 1, :] = part[n : n + 1, :] + diagonals(
                    products[spots] * upper + inners[spots] * keep
                )
        conv_v = conv_s[...]
        back_v = back_s[...]
        mixed_out[span, :] = (feat[0] * conv_v).astype(BF)
        grad = [
            (up * conv_v).astype(BF),
            (back_v * feat[2]).astype(BF),
            (back_v * feat[1]).astype(BF),
        ]
        for j in range(3):
            grads[j, span] = grad[j]
            moved = nt(shifts[...], grad[j])
            raw = nt(eye, x[j, span])
            head = nt(take_head, grad[j])
            heads[j, :, span] = head.astype(BF)
            columns = []
            for lag in range(short):
                piece = moved[lag * tok : (lag + 1) * tok]
                column = jnp.sum(raw * piece, axis=0, keepdims=True)
                if lag > 0:
                    cross = head * pads[j][EDGE - lag : 2 * EDGE - lag]
                    column = column + jnp.sum(cross, axis=0, keepdims=True)
                columns.append(column)
            columns += [jnp.zeros((1, BLOCK), F32)] * (EDGE - short)
            stacked = jnp.concatenate(columns, axis=0)
            for h in range(BLOCK // TILE):
                at = base + per + (j * (BLOCK // TILE) + h) * EDGE
                sums[at : at + EDGE, :] = stacked[:, h * TILE : (h + 1) * TILE]


def streams_kernel(marks, w, grads, next_heads, out, shifts):
    short = w.shape[1]
    tok = marks.shape[1]
    seg_col, seg_row, row, col = segments(marks)
    fill_shifts(shifts, seg_col == seg_row, row - col, short)
    open_end = seg_col[tok - EDGE :, 0:BLOCK] == seg_col[tok - 1 : tok, 0:BLOCK]
    eye = identity(BLOCK)
    for lo in range(0, grads.shape[1], BLOCK):
        span = slice(lo, lo + BLOCK)
        for j in range(3):
            taps = tap_columns(w, j, span)
            total = nn(weighted(grads[j, span], taps, short), shifts[...])
            pad = next_heads[j, :, span].astype(F32)
            pad = jnp.concatenate([jnp.zeros_like(pad), pad], axis=0)
            fix = jnp.where(open_end, border_sum(w, j, span, pad, False), 0.0)
            wide = jnp.concatenate([jnp.zeros((TILE - EDGE, BLOCK), F32), fix], axis=0)
            out[j, span, 0:TILE] = total[:, 0:TILE].astype(BF)
            out[j, span, TILE:] = (total[:, TILE:] + nt(eye, wide.astype(BF))).astype(BF)


def merge_kernel(me, pieces, out):
    far = out.shape[0]
    tp = me.shape[0]
    rows = pieces.shape[1]
    rest = pieces.shape[0] // tp
    total = pieces[0:tp].astype(F32)
    for z in range(1, rest):
        total = total + pieces[z * tp : (z + 1) * tp].astype(F32)
    own = jnp.sum(total * me[...], axis=0)
    square = jnp.broadcast_to(jnp.sum(total * total), (out.shape[1] - rows, TILE))
    for i in range(far):
        out[i, 0:rows] = own
        out[i, rows:] = square


def scale_kernel(entries, shares, grad_long, grad_short):
    rows = shares.shape[1] - EDGE
    mean = jnp.sum(shares[:, rows, 0:1]) / entries
    wide = jnp.broadcast_to(mean, (EDGE, TILE))
    scale = jnp.minimum(1.0, 1.0 / jnp.sqrt(wide + 1e-06))[0:1]
    total = jnp.concatenate([shares[i, 0:rows] for i in range(shares.shape[0])], axis=0)
    short = grad_short.shape[1]
    members = grad_short.shape[2] // grad_long.shape[0]
    per = BLOCK // members
    stride = per + 3 * (BLOCK // TILE) * EDGE
    for b in range(grad_short.shape[2] // BLOCK):
        base = b * stride
        grad_long[b * per : (b + 1) * per, :] = total[base : base + per, :] * scale
        for j in range(3):
            for h in range(BLOCK // TILE):
                at = base + per + (j * (BLOCK // TILE) + h) * EDGE
                lane = b * BLOCK + h * TILE
                grad_short[j, :, lane : lane + TILE] = total[at : at + short, :] * scale


def call(kernel, outs, scratch, *args, limit=LIMIT):
    return pl.pallas_call(
        kernel,
        in_specs=[pl.BlockSpec(memory_space=pltpu.VMEM) for _ in args],
        out_specs=[pl.BlockSpec(memory_space=pltpu.VMEM) for _ in outs],
        out_shape=[jax.ShapeDtypeStruct(s, d) for s, d in outs],
        scratch_shapes=scratch,
        compiler_params=pltpu.CompilerParams(vmem_limit_bytes=limit),
        cost_estimate=pl.CostEstimate(
            flops=2 * 10**9, bytes_accessed=8 * 10**6, transcendentals=0
        ),
    )(*args)


def step_forward(block, size):
    return lax.ppermute(block, SEQ, [(i, i + 1) for i in range(size - 1)])


def step_back(block, size):
    return lax.ppermute(block, SEQ, [(i + 1, i) for i in range(size - 1)])


def exchange(pieces, axes):
    return lax.all_to_all(pieces, axes, 0, 0)


def local(streams, short_taps, long_taps, doc_marks, upstream):
    chan, tok = streams.shape[1:]
    groups, taps = long_taps.shape
    short = short_taps.shape[2]
    members = chan // groups
    size = lax.axis_size(SEQ)
    w = jnp.transpose(short_taps, (0, 2, 1))
    marks = doc_marks.reshape(1, tok)
    shifts = ((short * tok, tok), BF)
    whole = ((3, chan, tok), BF)
    tiles = chan // TILE

    late = ((chan, TILE), BF)
    feats, next_pack, last_pack, moves, mixed_late, gate_late = call(
        feats_kernel,
        [
            whole, ((chan + 2 * tiles * PACK, TILE), BF), ((chan + tiles * PACK, TILE), BF),
            shifts, late, late,
        ],
        [],
        marks, streams, w, upstream,
        limit=FIRST_LIMIT,
    )
    from_last = step_forward(next_pack, size)
    from_next = step_back(last_pack, size)

    half = ((chan, TILE), F32)
    conv, back, part = call(
        functools.partial(own_kernel, members),
        [half, half, ((groups, taps), F32)],
        [],
        marks, mixed_late, gate_late, long_taps,
    )
    rows = groups + 3 * tiles * EDGE
    mixed_out, feat_grad, heads, sums = call(
        functools.partial(halo_kernel, members),
        [((chan, tok), BF), whole, ((3, EDGE, chan), BF), ((rows, TILE), F32)],
        [pltpu.VMEM((BLOCK, tok), F32), pltpu.VMEM((BLOCK, tok), F32)],
        marks, streams, w, feats, upstream, from_last, from_next, conv, back, long_taps, part, moves,
    )
    next_heads = step_back(heads, size)

    cube = lax.axis_size(CUBE)
    tp = lax.axis_size(TP)
    far = tp * lax.axis_size("zh")
    share = rows // cube
    mine = jnp.sum(exchange(sums.reshape(cube, share, TILE), CUBE), axis=0).astype(BF)
    mine, feat_grad, next_heads = lax.optimization_barrier((mine, feat_grad, next_heads))
    pieces = exchange(jnp.broadcast_to(mine, (far,) + mine.shape), FAR)
    (grad_streams,) = call(
        streams_kernel, [whole], [pltpu.VMEM(*shifts)], marks, w, feat_grad, next_heads
    )
    pieces, grad_streams = lax.optimization_barrier((pieces, grad_streams))
    me = jnp.where(jnp.arange(tp) == lax.axis_index(TP), 1.0, 0.0).astype(F32)
    me = jnp.broadcast_to(me[:, None, None], (tp, 1, TILE))
    (payload,) = call(merge_kernel, [((cube, share + EDGE, TILE), F32)], [], me, pieces)
    shares = exchange(payload, CUBE)
    entries = tp * (groups * taps + 3 * chan * short)
    grad_long, grad_short = call(
        functools.partial(scale_kernel, entries),
        [((groups, taps), F32), ((3, short, chan), F32)],
        [],
        shares,
    )
    return (mixed_out, grad_streams, grad_long, jnp.transpose(grad_short, (0, 2, 1)))


def solution(mesh):
    fine = Mesh(mesh.devices.reshape(4, 4, 4, 4, 2), ("x", "zh", "zl", "y", "c"))
    in_specs = (P(None, TP, SEQ), P(None, TP, None), P(TP, None), P(SEQ), P(TP, SEQ))
    out_specs = (P(TP, SEQ), P(None, TP, SEQ), P(TP, None), P(None, TP, None))
    return jax.shard_map(local, mesh=fine, in_specs=in_specs, out_specs=out_specs, check_vma=False)
```

```python
import functools

import jax
import jax.numpy as jnp
from jax import lax
from jax.experimental import pallas as pl
from jax.experimental.pallas import tpu as pltpu
from jax.sharding import Mesh
from jax.sharding import PartitionSpec as P

BF = jnp.bfloat16
F32 = jnp.float32
SEQ = ("x", "zh", "zl")
TP = ("y", "c")
CUBE = ("x", "zl")
FAR = ("zh", "y", "c")
TILE = 128
EDGE = 8
PACK = 16
BLOCK = 256
LIMIT = 24 * 1024 * 1024
FIRST_LIMIT = 57 * 1024 * 1024


def nt(left, right):
    return lax.dot_general(left, right, (((1,), (1,)), ((), ())), preferred_element_type=F32)


def nn(left, right):
    return lax.dot_general(left, right, (((1,), (0,)), ((), ())), preferred_element_type=F32)


def ones_where(keep):
    return jnp.where(keep, 1.0, 0.0).astype(BF)


def grid_of(rows, cols):
    return (
        lax.broadcasted_iota(jnp.int32, (rows, cols), 0),
        lax.broadcasted_iota(jnp.int32, (rows, cols), 1),
    )


def segments(marks):
    tok = marks.shape[1]
    row, col = grid_of(tok, tok)
    lower = ones_where(col <= row)
    wide = jnp.broadcast_to(jnp.where(marks[...] == 1, 1.0, 0.0), (tok, tok)).astype(BF)
    return nt(lower, wide), nt(wide, lower), row, col


def identity(size):
    row, col = grid_of(size, size)
    return ones_where(row == col)


def reversal():
    row, col = grid_of(TILE, TILE)
    return ones_where(row + col == TILE - 1)


def fill_shifts(shifts, same, offset, short):
    tok = same.shape[0]
    for lag in range(short):
        shifts[lag * tok : (lag + 1) * tok, :] = ones_where((offset == lag) & same)


def tap_columns(w, j, span):
    short = w.shape[1]
    wide = jnp.concatenate(
        [w[j, :, span], jnp.zeros((EDGE - short, BLOCK), F32)], axis=0
    )
    return jnp.transpose(wide)


def weighted(values, taps, short):
    parts = []
    values = values.astype(F32)
    for lag in range(short):
        tap = jnp.broadcast_to(taps[:, lag : lag + 1], (BLOCK, TILE))
        for lo in range(0, values.shape[1], TILE):
            parts.append((values[:, lo : lo + TILE] * tap).astype(BF))
    return jnp.concatenate(parts, axis=1)


def edge_rows(packed, first, j, lo):
    rows = []
    for tile in range(lo // TILE, (lo + BLOCK) // TILE):
        at = first + (2 * tile + j // 2) * PACK
        rows.append(packed[at : at + PACK, :].astype(F32)[(j % 2) * EDGE : (j % 2 + 1) * EDGE])
    return jnp.concatenate(rows, axis=1)


def border_sum(w, j, span, pad, forward):
    total = None
    for lag in range(1, w.shape[1]):
        lo = EDGE - lag if forward else lag
        term = w[j, lag : lag + 1, span] * pad[lo : lo + EDGE]
        total = term if total is None else total + term
    return total


def after(rows):
    return jnp.concatenate([rows, jnp.zeros_like(rows)], axis=0)


def at_front(rows, eye):
    wide = jnp.concatenate([rows, jnp.zeros((TILE - EDGE, rows.shape[1]), F32)], axis=0)
    return nt(eye, wide.astype(BF))


def feats_kernel(marks, x, w, ups, feats, next_pack, last_pack, mixed_late, gate_late, shifts):
    short = w.shape[1]
    chan, tok = ups.shape
    seg_col, seg_row, row, col = segments(marks)
    fill_shifts(shifts, seg_col == seg_row, col - row, short)
    first = seg_row[0:1, :]
    open_end = first == first[:, tok - 1 : tok]
    open_start = first == 0
    head_row, head_col = grid_of(PACK, tok)
    take_tail = ones_where((head_col == tok - EDGE + head_row) & open_end & (head_row < EDGE))
    take_head = ones_where((head_col == head_row) & (head_row < EDGE) & open_start)
    for lo in range(0, chan, BLOCK):
        span = slice(lo, lo + BLOCK)
        outs = []
        tails = []
        for j in range(3):
            raw = x[j, span]
            taps = tap_columns(w, j, span)
            out = nn(weighted(raw, taps, short), shifts[...]).astype(BF)
            feats[j, span] = out
            outs.append(out.astype(F32))
            tails.append(nt(take_tail, raw)[0:EDGE])
        tails.append(jnp.zeros_like(tails[0]))
        mixed = outs[1][:, tok - TILE :] * outs[2][:, tok - TILE :]
        mixed_late[span, :] = mixed.astype(BF)
        next_pack[span, :] = jnp.where(open_end[:, tok - TILE :], mixed, 0.0).astype(BF)
        up = ups[span]
        gate = up.astype(F32) * outs[0]
        gate_late[span, :] = gate[:, tok - TILE :].astype(BF)
        last_pack[span, :] = jnp.where(open_start[:, 0:TILE], gate[:, 0:TILE], 0.0).astype(BF)
        heads = nt(take_head, up).astype(BF)
        pairs = [
            jnp.concatenate([tails[p], tails[p + 1]], axis=0).astype(BF) for p in (0, 2)
        ]
        for h in range(0, BLOCK, TILE):
            tile = (lo + h) // TILE
            at = chan + tile * PACK
            last_pack[at : at + PACK, :] = heads[:, h : h + TILE]
            for p in range(2):
                at = chan + (2 * tile + p) * PACK
                next_pack[at : at + PACK, :] = pairs[p][:, h : h + TILE]


def circulant(filt, g):
    row = filt[g : g + 1, :].astype(BF).astype(F32)
    wide = jnp.broadcast_to(row, (TILE, TILE))
    return pltpu.roll(wide, 0, 1, stride=1, stride_axis=0).astype(BF)


def turned_filters(filt):
    row, col = grid_of(TILE, TILE)
    return nn(filt[...].astype(BF), ones_where((row + col == TILE) | (row + col == 0)))


def spread(block, picks):
    return jnp.concatenate([block * pick for pick in picks], axis=0)


def diagonals(product):
    moved = pltpu.roll(product, 1, 1, stride=1, stride_axis=0)
    return jnp.sum(moved, axis=0, keepdims=True)


def members_mask(start, members):
    row, col = grid_of(TILE, TILE)
    return ones_where((col >= start) & (col < start + members))


def own_kernel(members, marks, mixed_late, gate_late, filt, conv, back, part):
    chan = mixed_late.shape[0]
    tok = marks.shape[1]
    seg_col, seg_row, row, col = segments(marks)
    flip = reversal()
    s = slice(TILE, tok)
    keep_bf = ones_where((seg_col[s, s] == seg_row[s, s]) & (col[s, s] >= row[s, s]))
    keep = nn(flip, keep_bf)
    keep_tbf = ones_where((seg_col[s, s] == seg_row[s, s]) & (col[s, s] <= row[s, s]))
    back_filt = turned_filters(filt)
    picks = [members_mask(p, members) for p in range(0, TILE, members)]
    for lo in range(0, chan, BLOCK):
        span = slice(lo, lo + BLOCK)
        mixed = mixed_late[span]
        gate = gate_late[span]
        mixed_t = nt(flip, mixed).astype(BF)
        for cb in range(BLOCK // TILE):
            chans = slice(cb * TILE, (cb + 1) * TILE)
            products = nn(spread(mixed_t[:, chans], picks), gate[chans])
            for k in range(len(picks)):
                g = cb * len(picks) + k
                n = lo // members + g
                rows = slice(g * members, (g + 1) * members)
                at = slice(lo + g * members, lo + (g + 1) * members)
                conv[at, :] = nn(mixed[rows], circulant(filt, n) * keep_bf)
                back[at, :] = nn(gate[rows], circulant(back_filt, n) * keep_tbf)
                part[n : n + 1, :] = diagonals(products[k * TILE : (k + 1) * TILE] * keep)


def halo_kernel(
    members, marks, x, w, feats, ups, from_last, from_next, conv, back, filt, part,
    mixed_out, grads, heads, sums_out, shifts, conv_s, back_s, sums,
):
    short = w.shape[1]
    chan, tok = ups.shape
    seg_col, seg_row, row, col = segments(marks)
    fill_shifts(shifts, seg_col == seg_row, col - row, short)
    eye = identity(BLOCK)
    flip = reversal()
    first = seg_row[0:1, :]
    middle = first[:, TILE - 1 : TILE]
    last = first[:, tok - 1 : tok]
    from_start = [
        jnp.where(first[:, 0:TILE] == 0, 1.0, 0.0),
        jnp.where(first[:, TILE:] == middle, 1.0, 0.0),
    ]
    to_end = [
        jnp.where(first[:, 0:TILE] == middle, 1.0, 0.0),
        jnp.where(first[:, TILE:] == last, 1.0, 0.0),
    ]
    row_t, col_t = grid_of(TILE, TILE)
    upper_bf = ones_where(col_t < row_t)
    upper = jnp.where(col_t + row_t < TILE - 1, 1.0, 0.0)
    s = slice(0, TILE)
    keep_bf = ones_where((seg_col[s, s] == seg_row[s, s]) & (col[s, s] >= row[s, s]))
    keep = nn(flip, keep_bf)
    keep_tbf = ones_where((seg_col[s, s] == seg_row[s, s]) & (col[s, s] <= row[s, s]))
    upper_tbf = ones_where(col_t > row_t)
    back_filt = turned_filters(filt)
    open_start = seg_col[0:EDGE, 0:BLOCK] == 0
    head_row, head_col = grid_of(EDGE, tok)
    take_head = ones_where((head_col == head_row) & (first == 0))
    take_tail = ones_where((head_col == tok - EDGE + head_row) & (first == last))
    picks = [members_mask(p, members) for p in range(0, TILE, members)]
    per = BLOCK // members
    stride = per + 3 * (BLOCK // TILE) * EDGE
    for lo in range(0, chan, BLOCK):
        span = slice(lo, lo + BLOCK)
        pads = [after(edge_rows(from_last, chan, j, lo)) for j in range(3)]
        feat = []
        for j in range(3):
            fix = jnp.where(open_start, border_sum(w, j, span, pads[j], True), 0.0)
            head = (feats[j, span, 0:TILE].astype(F32) + at_front(fix, eye)).astype(BF)
            feat.append(jnp.concatenate([head, feats[j, span, TILE:]], axis=1).astype(F32))
        up = ups[span].astype(F32)
        gate = up * feat[0]
        mixed = feat[1][:, 0:TILE] * feat[2][:, 0:TILE]
        mixed_b = mixed.astype(BF)
        gate_b = gate[:, 0:TILE].astype(BF)
        mixed0 = (mixed * to_end[0]).astype(BF)
        gate0 = (gate[:, 0:TILE] * from_start[0]).astype(BF)
        gate1 = (gate[:, TILE:] * from_start[1]).astype(BF)
        mixed_h = from_last[span]
        beyond = border_sum(w, 0, span, after(nt(take_tail, x[0, span])), True)
        ups_head = jnp.concatenate(
            [
                from_next[at : at + PACK, :].astype(F32)[0:EDGE]
                for at in range(chan + lo // TILE * PACK, chan + (lo + BLOCK) // TILE * PACK, PACK)
            ],
            axis=1,
        )
        gate_h = (from_next[span].astype(F32) + at_front(ups_head * beyond, eye)).astype(BF)
        lead_t = nt(flip, mixed_h).astype(BF)
        mixed_t = nt(flip, mixed0).astype(BF)
        whole_t = nt(flip, mixed_b).astype(BF)
        base = lo // BLOCK * stride
        for cb in range(BLOCK // TILE):
            chans = slice(cb * TILE, (cb + 1) * TILE)
            both = jnp.concatenate(
                [spread(lead_t[:, chans], picks), spread(mixed_t[:, chans], picks)], axis=1
            )
            products = nn(both, jnp.concatenate([gate0[chans], gate1[chans]], axis=0))
            inners = nn(spread(whole_t[:, chans], picks), gate_b[chans])
            for k in range(len(picks)):
                g = cb * len(picks) + k
                n = lo // members + g
                table = circulant(filt, n)
                diag = table * keep_bf
                table = table * upper_bf
                turned = circulant(back_filt, n)
                diag_b = turned * keep_tbf
                turned = turned * upper_tbf
                rows = slice(g * members, (g + 1) * members)
                at = slice(lo + g * members, lo + (g + 1) * members)
                ahead = nn(
                    jnp.concatenate([mixed_h[rows], mixed0[rows], mixed_b[rows]], axis=0),
                    jnp.concatenate([table, diag], axis=1),
                )
                conv_s[rows, 0:TILE] = (
                    ahead[2 * members :, TILE:] + ahead[0:members, 0:TILE] * from_start[0]
                )
                conv_s[rows, TILE:] = (
                    conv[at] + ahead[members : 2 * members, 0:TILE] * from_start[1]
                )
                behind = nn(
                    jnp.concatenate([gate1[rows], gate_h[rows], gate_b[rows]], axis=0),
                    jnp.concatenate([turned, diag_b], axis=1),
                )
                back_s[rows, 0:TILE] = (
                    behind[2 * members :, TILE:] + behind[0:members, 0:TILE] * to_end[0]
                )
                back_s[rows, TILE:] = (
                    back[at] + behind[members : 2 * members, 0:TILE] * to_end[1]
                )
                spots = slice(k * TILE, (k + 1) * TILE)
                sums[base + g : base + g + 1, :] = part[n : n + 1, :] + diagonals(
                    products[spots] * upper + inners[spots] * keep
                )
        conv_v = conv_s[...]
        back_v = back_s[...]
        mixed_out[span, :] = (feat[0] * conv_v).astype(BF)
        grad = [
            (up * conv_v).astype(BF),
            (back_v * feat[2]).astype(BF),
            (back_v * feat[1]).astype(BF),
        ]
        for j in range(3):
            grads[j, span] = grad[j]
            moved = nt(shifts[...], grad[j])
            raw = nt(eye, x[j, span])
            head = nt(take_head, grad[j])
            heads[j, :, span] = head.astype(BF)
            columns = []
            for lag in range(short):
                piece = moved[lag * tok : (lag + 1) * tok]
                column = jnp.sum(raw * piece, axis=0, keepdims=True)
                if lag > 0:
                    cross = head * pads[j][EDGE - lag : 2 * EDGE - lag]
                    column = column + jnp.sum(cross, axis=0, keepdims=True)
                columns.append(column)
            columns += [jnp.zeros((1, BLOCK), F32)] * (EDGE - short)
            stacked = jnp.concatenate(columns, axis=0)
            for h in range(BLOCK // TILE):
                at = base + per + (j * (BLOCK // TILE) + h) * EDGE
                sums[at : at + EDGE, :] = stacked[:, h * TILE : (h + 1) * TILE]
    sums_out[...] = sums[...].astype(BF)


def streams_kernel(marks, w, grads, next_heads, out, shifts):
    short = w.shape[1]
    tok = marks.shape[1]
    seg_col, seg_row, row, col = segments(marks)
    fill_shifts(shifts, seg_col == seg_row, row - col, short)
    open_end = seg_col[tok - EDGE :, 0:BLOCK] == seg_col[tok - 1 : tok, 0:BLOCK]
    eye = identity(BLOCK)
    for lo in range(0, grads.shape[1], BLOCK):
        span = slice(lo, lo + BLOCK)
        for j in range(3):
            taps = tap_columns(w, j, span)
            total = nn(weighted(grads[j, span], taps, short), shifts[...])
            pad = next_heads[j, :, span].astype(F32)
            pad = jnp.concatenate([jnp.zeros_like(pad), pad], axis=0)
            fix = jnp.where(open_end, border_sum(w, j, span, pad, False), 0.0)
            wide = jnp.concatenate([jnp.zeros((TILE - EDGE, BLOCK), F32), fix], axis=0)
            out[j, span, 0:TILE] = total[:, 0:TILE].astype(BF)
            out[j, span, TILE:] = (total[:, TILE:] + nt(eye, wide.astype(BF))).astype(BF)


def merge_kernel(me, pieces, out):
    far = out.shape[0]
    tp = me.shape[0]
    rows = pieces.shape[1]
    rest = pieces.shape[0] // tp
    total = pieces[0:tp].astype(F32)
    for z in range(1, rest):
        total = total + pieces[z * tp : (z + 1) * tp].astype(F32)
    own = jnp.sum(total * me[...], axis=0).astype(BF)
    square = jnp.broadcast_to(jnp.sum(total * total), (PACK, TILE))
    high = square.astype(BF).astype(F32)
    row, _ = grid_of(PACK, TILE)
    square = jnp.where(row == 0, high, jnp.where(row == 1, square - high, 0.0)).astype(BF)
    for i in range(far):
        out[i, 0:rows] = own
        out[i, rows:] = square


def scale_kernel(entries, shares, grad_long, grad_short):
    rows = shares.shape[1] - PACK
    extra = shares[:, rows:].astype(F32)
    mean = jnp.sum(extra[:, :, 0:1]) / entries
    wide = jnp.broadcast_to(mean, (EDGE, TILE))
    scale = jnp.minimum(1.0, 1.0 / jnp.sqrt(wide + 1e-06))[0:1]
    total = jnp.concatenate([shares[i, 0:rows].astype(F32) for i in range(shares.shape[0])], axis=0)
    short = grad_short.shape[1]
    members = grad_short.shape[2] // grad_long.shape[0]
    per = BLOCK // members
    stride = per + 3 * (BLOCK // TILE) * EDGE
    for b in range(grad_short.shape[2] // BLOCK):
        base = b * stride
        grad_long[b * per : (b + 1) * per, :] = total[base : base + per, :] * scale
        for j in range(3):
            for h in range(BLOCK // TILE):
                at = base + per + (j * (BLOCK // TILE) + h) * EDGE
                lane = b * BLOCK + h * TILE
                grad_short[j, :, lane : lane + TILE] = total[at : at + short, :] * scale


def call(kernel, outs, scratch, *args, limit=LIMIT):
    return pl.pallas_call(
        kernel,
        in_specs=[pl.BlockSpec(memory_space=pltpu.VMEM) for _ in args],
        out_specs=[pl.BlockSpec(memory_space=pltpu.VMEM) for _ in outs],
        out_shape=[jax.ShapeDtypeStruct(s, d) for s, d in outs],
        scratch_shapes=scratch,
        compiler_params=pltpu.CompilerParams(vmem_limit_bytes=limit),
        cost_estimate=pl.CostEstimate(
            flops=2 * 10**9, bytes_accessed=8 * 10**6, transcendentals=0
        ),
    )(*args)


def step_forward(block, size):
    return lax.ppermute(block, SEQ, [(i, i + 1) for i in range(size - 1)])


def step_back(block, size):
    return lax.ppermute(block, SEQ, [(i + 1, i) for i in range(size - 1)])


def exchange(pieces, axes):
    return lax.all_to_all(pieces, axes, 0, 0)


def local(streams, short_taps, long_taps, doc_marks, upstream):
    chan, tok = streams.shape[1:]
    groups, taps = long_taps.shape
    short = short_taps.shape[2]
    members = chan // groups
    size = lax.axis_size(SEQ)
    w = jnp.transpose(short_taps, (0, 2, 1))
    marks = doc_marks.reshape(1, tok)
    shifts = ((short * tok, tok), BF)
    whole = ((3, chan, tok), BF)
    tiles = chan // TILE

    late = ((chan, TILE), BF)
    feats, next_pack, last_pack, mixed_late, gate_late = call(
        feats_kernel,
        [
            whole, ((chan + 2 * tiles * PACK, TILE), BF), ((chan + tiles * PACK, TILE), BF),
            late, late,
        ],
        [pltpu.VMEM(*shifts)],
        marks, streams, w, upstream,
        limit=FIRST_LIMIT,
    )
    from_last = step_forward(next_pack, size)
    from_next = step_back(last_pack, size)

    half = ((chan, TILE), F32)
    conv, back, part = call(
        functools.partial(own_kernel, members),
        [half, half, ((groups, taps), F32)],
        [],
        marks, mixed_late, gate_late, long_taps,
    )
    rows = groups + 3 * tiles * EDGE
    mixed_out, feat_grad, heads, sums = call(
        functools.partial(halo_kernel, members),
        [((chan, tok), BF), whole, ((3, EDGE, chan), BF), ((rows, TILE), BF)],
        [
            pltpu.VMEM(*shifts), pltpu.VMEM((BLOCK, tok), F32), pltpu.VMEM((BLOCK, tok), F32),
            pltpu.VMEM((rows, TILE), F32),
        ],
        marks, streams, w, feats, upstream, from_last, from_next, conv, back, long_taps, part,
    )
    next_heads = step_back(heads, size)

    cube = lax.axis_size(CUBE)
    tp = lax.axis_size(TP)
    far = tp * lax.axis_size("zh")
    share = rows // cube
    mine = exchange(sums.reshape(cube, share, TILE), CUBE).astype(F32)
    mine = jnp.sum(mine, axis=0).astype(BF)
    mine, feat_grad, next_heads = lax.optimization_barrier((mine, feat_grad, next_heads))
    pieces = exchange(jnp.broadcast_to(mine, (far,) + mine.shape), FAR)
    (grad_streams,) = call(
        streams_kernel, [whole], [pltpu.VMEM(*shifts)], marks, w, feat_grad, next_heads
    )
    pieces, grad_streams = lax.optimization_barrier((pieces, grad_streams))
    me = jnp.where(jnp.arange(tp) == lax.axis_index(TP), 1.0, 0.0).astype(F32)
    me = jnp.broadcast_to(me[:, None, None], (tp, 1, TILE))
    (payload,) = call(merge_kernel, [((cube, share + PACK, TILE), BF)], [], me, pieces)
    shares = exchange(payload, CUBE)
    entries = tp * (groups * taps + 3 * chan * short)
    grad_long, grad_short = call(
        functools.partial(scale_kernel, entries),
        [((groups, taps), F32), ((3, short, chan), F32)],
        [],
        shares,
    )
    return (mixed_out, grad_streams, grad_long, jnp.transpose(grad_short, (0, 2, 1)))


def solution(mesh):
    fine = Mesh(mesh.devices.reshape(4, 4, 4, 4, 2), ("x", "zh", "zl", "y", "c"))
    in_specs = (P(None, TP, SEQ), P(None, TP, None), P(TP, None), P(SEQ), P(TP, SEQ))
    out_specs = (P(TP, SEQ), P(None, TP, SEQ), P(TP, None), P(None, TP, None))
    return jax.shard_map(local, mesh=fine, in_specs=in_specs, out_specs=out_specs, check_vma=False)
```

```python
import functools

import jax
import jax.numpy as jnp
from jax import lax
from jax.experimental import pallas as pl
from jax.experimental.pallas import tpu as pltpu
from jax.sharding import Mesh
from jax.sharding import PartitionSpec as P

BF = jnp.bfloat16
F32 = jnp.float32
SEQ = ("x", "zh", "zl")
TP = ("y", "c")
CUBE = ("x", "zl")
FAR = ("zh", "y", "c")
TILE = 128
EDGE = 8
PACK = 16
BLOCK = 256
LIMIT = 24 * 1024 * 1024
FIRST_LIMIT = 57 * 1024 * 1024


def nt(left, right):
    return lax.dot_general(left, right, (((1,), (1,)), ((), ())), preferred_element_type=F32)


def nn(left, right):
    return lax.dot_general(left, right, (((1,), (0,)), ((), ())), preferred_element_type=F32)


def ones_where(keep):
    return jnp.where(keep, 1.0, 0.0).astype(BF)


def grid_of(rows, cols):
    return (
        lax.broadcasted_iota(jnp.int32, (rows, cols), 0),
        lax.broadcasted_iota(jnp.int32, (rows, cols), 1),
    )


def segments(marks):
    tok = marks.shape[1]
    row, col = grid_of(tok, tok)
    lower = ones_where(col <= row)
    wide = jnp.broadcast_to(jnp.where(marks[...] == 1, 1.0, 0.0), (tok, tok)).astype(BF)
    return nt(lower, wide), nt(wide, lower), row, col


def identity(size):
    row, col = grid_of(size, size)
    return ones_where(row == col)


def reversal():
    row, col = grid_of(TILE, TILE)
    return ones_where(row + col == TILE - 1)


def fill_shifts(shifts, same, offset, short):
    tok = same.shape[0]
    for lag in range(short):
        shifts[lag * tok : (lag + 1) * tok, :] = ones_where((offset == lag) & same)


def tap_columns(w, j, span):
    short = w.shape[1]
    wide = jnp.concatenate(
        [w[j, :, span], jnp.zeros((EDGE - short, BLOCK), F32)], axis=0
    )
    return jnp.transpose(wide)


def weighted(values, taps, short):
    parts = []
    values = values.astype(F32)
    for lag in range(short):
        tap = jnp.broadcast_to(taps[:, lag : lag + 1], (BLOCK, TILE))
        for lo in range(0, values.shape[1], TILE):
            parts.append((values[:, lo : lo + TILE] * tap).astype(BF))
    return jnp.concatenate(parts, axis=1)


def edge_rows(packed, first, j, lo):
    rows = []
    for tile in range(lo // TILE, (lo + BLOCK) // TILE):
        at = first + (2 * tile + j // 2) * PACK
        rows.append(packed[at : at + PACK, :].astype(F32)[(j % 2) * EDGE : (j % 2 + 1) * EDGE])
    return jnp.concatenate(rows, axis=1)


def border_sum(w, j, span, pad, forward):
    total = None
    for lag in range(1, w.shape[1]):
        lo = EDGE - lag if forward else lag
        term = w[j, lag : lag + 1, span] * pad[lo : lo + EDGE]
        total = term if total is None else total + term
    return total


def after(rows):
    return jnp.concatenate([rows, jnp.zeros_like(rows)], axis=0)


def at_front(rows, eye):
    wide = jnp.concatenate([rows, jnp.zeros((TILE - EDGE, rows.shape[1]), F32)], axis=0)
    return nt(eye, wide.astype(BF))


def feats_kernel(marks, x, w, ups, feats, next_pack, last_pack, mixed_late, gate_late, shifts):
    short = w.shape[1]
    chan, tok = ups.shape
    seg_col, seg_row, row, col = segments(marks)
    fill_shifts(shifts, seg_col == seg_row, col - row, short)
    first = seg_row[0:1, :]
    open_end = first == first[:, tok - 1 : tok]
    open_start = first == 0
    head_row, head_col = grid_of(PACK, tok)
    take_tail = ones_where((head_col == tok - EDGE + head_row) & open_end & (head_row < EDGE))
    take_head = ones_where((head_col == head_row) & (head_row < EDGE) & open_start)
    for lo in range(0, chan, BLOCK):
        span = slice(lo, lo + BLOCK)
        outs = []
        tails = []
        for j in range(3):
            raw = x[j, span]
            taps = tap_columns(w, j, span)
            out = nn(weighted(raw, taps, short), shifts[...]).astype(BF)
            feats[j, span] = out
            outs.append(out.astype(F32))
            tails.append(nt(take_tail, raw)[0:EDGE])
        tails.append(jnp.zeros_like(tails[0]))
        mixed = outs[1][:, tok - TILE :] * outs[2][:, tok - TILE :]
        mixed_late[span, :] = mixed.astype(BF)
        next_pack[span, :] = jnp.where(open_end[:, tok - TILE :], mixed, 0.0).astype(BF)
        up = ups[span]
        gate = up.astype(F32) * outs[0]
        gate_late[span, :] = gate[:, tok - TILE :].astype(BF)
        last_pack[span, :] = jnp.where(open_start[:, 0:TILE], gate[:, 0:TILE], 0.0).astype(BF)
        heads = nt(take_head, up).astype(BF)
        pairs = [
            jnp.concatenate([tails[p], tails[p + 1]], axis=0).astype(BF) for p in (0, 2)
        ]
        for h in range(0, BLOCK, TILE):
            tile = (lo + h) // TILE
            at = chan + tile * PACK
            last_pack[at : at + PACK, :] = heads[:, h : h + TILE]
            for p in range(2):
                at = chan + (2 * tile + p) * PACK
                next_pack[at : at + PACK, :] = pairs[p][:, h : h + TILE]


def circulant(filt, g):
    row = filt[g : g + 1, :].astype(BF).astype(F32)
    wide = jnp.broadcast_to(row, (TILE, TILE))
    return pltpu.roll(wide, 0, 1, stride=1, stride_axis=0).astype(BF)


def turned_filters(filt):
    row, col = grid_of(TILE, TILE)
    return nn(filt[...].astype(BF), ones_where((row + col == TILE) | (row + col == 0)))


def spread(block, picks):
    return jnp.concatenate([block * pick for pick in picks], axis=0)


def diagonals(product):
    moved = pltpu.roll(product, 1, 1, stride=1, stride_axis=0)
    return jnp.sum(moved, axis=0, keepdims=True)


def members_mask(start, members):
    row, col = grid_of(TILE, TILE)
    return ones_where((col >= start) & (col < start + members))


def own_kernel(members, marks, mixed_late, gate_late, filt, conv, back, part):
    chan = mixed_late.shape[0]
    tok = marks.shape[1]
    seg_col, seg_row, row, col = segments(marks)
    flip = reversal()
    s = slice(TILE, tok)
    keep_bf = ones_where((seg_col[s, s] == seg_row[s, s]) & (col[s, s] >= row[s, s]))
    keep = nn(flip, keep_bf)
    keep_tbf = ones_where((seg_col[s, s] == seg_row[s, s]) & (col[s, s] <= row[s, s]))
    back_filt = turned_filters(filt)
    picks = [members_mask(p, members) for p in range(0, TILE, members)]
    for lo in range(0, chan, BLOCK):
        span = slice(lo, lo + BLOCK)
        mixed = mixed_late[span]
        gate = gate_late[span]
        mixed_t = nt(flip, mixed).astype(BF)
        for cb in range(BLOCK // TILE):
            chans = slice(cb * TILE, (cb + 1) * TILE)
            products = nn(spread(mixed_t[:, chans], picks), gate[chans])
            for k in range(len(picks)):
                g = cb * len(picks) + k
                n = lo // members + g
                rows = slice(g * members, (g + 1) * members)
                at = slice(lo + g * members, lo + (g + 1) * members)
                conv[at, :] = nn(mixed[rows], circulant(filt, n) * keep_bf)
                back[at, :] = nn(gate[rows], circulant(back_filt, n) * keep_tbf)
                part[n : n + 1, :] = diagonals(products[k * TILE : (k + 1) * TILE] * keep)


def halo_kernel(
    members, marks, x, w, feats, ups, from_last, from_next, conv, back, filt, part,
    mixed_out, grads, heads, sums_out, shifts, conv_s, back_s, sums,
):
    short = w.shape[1]
    chan, tok = ups.shape
    seg_col, seg_row, row, col = segments(marks)
    fill_shifts(shifts, seg_col == seg_row, col - row, short)
    eye = identity(BLOCK)
    flip = reversal()
    first = seg_row[0:1, :]
    middle = first[:, TILE - 1 : TILE]
    last = first[:, tok - 1 : tok]
    from_start = [
        jnp.where(first[:, 0:TILE] == 0, 1.0, 0.0),
        jnp.where(first[:, TILE:] == middle, 1.0, 0.0),
    ]
    to_end = [
        jnp.where(first[:, 0:TILE] == middle, 1.0, 0.0),
        jnp.where(first[:, TILE:] == last, 1.0, 0.0),
    ]
    row_t, col_t = grid_of(TILE, TILE)
    upper_bf = ones_where(col_t < row_t)
    upper = jnp.where(col_t + row_t < TILE - 1, 1.0, 0.0)
    s = slice(0, TILE)
    keep_bf = ones_where((seg_col[s, s] == seg_row[s, s]) & (col[s, s] >= row[s, s]))
    keep = nn(flip, keep_bf)
    keep_tbf = ones_where((seg_col[s, s] == seg_row[s, s]) & (col[s, s] <= row[s, s]))
    upper_tbf = ones_where(col_t > row_t)
    back_filt = turned_filters(filt)
    open_start = seg_col[0:EDGE, 0:BLOCK] == 0
    head_row, head_col = grid_of(EDGE, tok)
    take_head = ones_where((head_col == head_row) & (first == 0))
    take_tail = ones_where((head_col == tok - EDGE + head_row) & (first == last))
    picks = [members_mask(p, members) for p in range(0, TILE, members)]
    per = BLOCK // members
    stride = per + 3 * (BLOCK // TILE) * EDGE
    for lo in range(0, chan, BLOCK):
        span = slice(lo, lo + BLOCK)
        pads = [after(edge_rows(from_last, chan, j, lo)) for j in range(3)]
        feat = []
        for j in range(3):
            fix = jnp.where(open_start, border_sum(w, j, span, pads[j], True), 0.0)
            head = (feats[j, span, 0:TILE].astype(F32) + at_front(fix, eye)).astype(BF)
            feat.append(jnp.concatenate([head, feats[j, span, TILE:]], axis=1).astype(F32))
        up = ups[span].astype(F32)
        gate = up * feat[0]
        mixed = feat[1][:, 0:TILE] * feat[2][:, 0:TILE]
        mixed_b = mixed.astype(BF)
        gate_b = gate[:, 0:TILE].astype(BF)
        mixed0 = (mixed * to_end[0]).astype(BF)
        gate0 = (gate[:, 0:TILE] * from_start[0]).astype(BF)
        gate1 = (gate[:, TILE:] * from_start[1]).astype(BF)
        mixed_h = from_last[span]
        beyond = border_sum(w, 0, span, after(nt(take_tail, x[0, span])), True)
        ups_head = jnp.concatenate(
            [
                from_next[at : at + PACK, :].astype(F32)[0:EDGE]
                for at in range(chan + lo // TILE * PACK, chan + (lo + BLOCK) // TILE * PACK, PACK)
            ],
            axis=1,
        )
        gate_h = (from_next[span].astype(F32) + at_front(ups_head * beyond, eye)).astype(BF)
        lead_t = nt(flip, mixed_h).astype(BF)
        mixed_t = nt(flip, mixed0).astype(BF)
        whole_t = nt(flip, mixed_b).astype(BF)
        base = lo // BLOCK * stride
        for cb in range(BLOCK // TILE):
            chans = slice(cb * TILE, (cb + 1) * TILE)
            both = jnp.concatenate(
                [spread(lead_t[:, chans], picks), spread(mixed_t[:, chans], picks)], axis=1
            )
            products = nn(both, jnp.concatenate([gate0[chans], gate1[chans]], axis=0))
            inners = nn(spread(whole_t[:, chans], picks), gate_b[chans])
            for k in range(len(picks)):
                g = cb * len(picks) + k
                n = lo // members + g
                table = circulant(filt, n)
                diag = table * keep_bf
                table = table * upper_bf
                turned = circulant(back_filt, n)
                diag_b = turned * keep_tbf
                turned = turned * upper_tbf
                rows = slice(g * members, (g + 1) * members)
                at = slice(lo + g * members, lo + (g + 1) * members)
                ahead = nn(
                    jnp.concatenate([mixed_h[rows], mixed0[rows], mixed_b[rows]], axis=0),
                    jnp.concatenate([table, diag], axis=1),
                )
                conv_s[rows, 0:TILE] = (
                    ahead[2 * members :, TILE:] + ahead[0:members, 0:TILE] * from_start[0]
                )
                conv_s[rows, TILE:] = (
                    conv[at] + ahead[members : 2 * members, 0:TILE] * from_start[1]
                )
                behind = nn(
                    jnp.concatenate([gate1[rows], gate_h[rows], gate_b[rows]], axis=0),
                    jnp.concatenate([turned, diag_b], axis=1),
                )
                back_s[rows, 0:TILE] = (
                    behind[2 * members :, TILE:] + behind[0:members, 0:TILE] * to_end[0]
                )
                back_s[rows, TILE:] = (
                    back[at] + behind[members : 2 * members, 0:TILE] * to_end[1]
                )
                spots = slice(k * TILE, (k + 1) * TILE)
                sums[base + g : base + g + 1, :] = part[n : n + 1, :] + diagonals(
                    products[spots] * upper + inners[spots] * keep
                )
        conv_v = conv_s[...]
        back_v = back_s[...]
        mixed_out[span, :] = (feat[0] * conv_v).astype(BF)
        grad = [
            (up * conv_v).astype(BF),
            (back_v * feat[2]).astype(BF),
            (back_v * feat[1]).astype(BF),
        ]
        for j in range(3):
            grads[j, span] = grad[j]
            moved = nt(shifts[...], grad[j])
            raw = nt(eye, x[j, span])
            head = nt(take_head, grad[j])
            heads[j, :, span] = head.astype(BF)
            columns = []
            for lag in range(short):
                piece = moved[lag * tok : (lag + 1) * tok]
                column = jnp.sum(raw * piece, axis=0, keepdims=True)
                if lag > 0:
                    cross = head * pads[j][EDGE - lag : 2 * EDGE - lag]
                    column = column + jnp.sum(cross, axis=0, keepdims=True)
                columns.append(column)
            columns += [jnp.zeros((1, BLOCK), F32)] * (EDGE - short)
            stacked = jnp.concatenate(columns, axis=0)
            for h in range(BLOCK // TILE):
                at = base + per + (j * (BLOCK // TILE) + h) * EDGE
                sums[at : at + EDGE, :] = stacked[:, h * TILE : (h + 1) * TILE]
    sums_out[...] = sums[...].astype(BF)


def streams_kernel(marks, w, grads, next_heads, out, shifts):
    short = w.shape[1]
    tok = marks.shape[1]
    seg_col, seg_row, row, col = segments(marks)
    fill_shifts(shifts, seg_col == seg_row, row - col, short)
    open_end = seg_col[tok - EDGE :, 0:BLOCK] == seg_col[tok - 1 : tok, 0:BLOCK]
    eye = identity(BLOCK)
    for lo in range(0, grads.shape[1], BLOCK):
        span = slice(lo, lo + BLOCK)
        for j in range(3):
            taps = tap_columns(w, j, span)
            total = nn(weighted(grads[j, span], taps, short), shifts[...])
            pad = next_heads[j, :, span].astype(F32)
            pad = jnp.concatenate([jnp.zeros_like(pad), pad], axis=0)
            fix = jnp.where(open_end, border_sum(w, j, span, pad, False), 0.0)
            wide = jnp.concatenate([jnp.zeros((TILE - EDGE, BLOCK), F32), fix], axis=0)
            out[j, span, 0:TILE] = total[:, 0:TILE].astype(BF)
            out[j, span, TILE:] = (total[:, TILE:] + nt(eye, wide.astype(BF))).astype(BF)


def merge_kernel(me, pieces, out):
    far = out.shape[0]
    tp = me.shape[0]
    rows = pieces.shape[1]
    rest = pieces.shape[0] // tp
    total = pieces[0:tp].astype(F32)
    for z in range(1, rest):
        total = total + pieces[z * tp : (z + 1) * tp].astype(F32)
    own = jnp.sum(total * me[...], axis=0).astype(BF)
    square = jnp.broadcast_to(jnp.sum(total * total), (PACK, TILE))
    high = square.astype(BF).astype(F32)
    row, _ = grid_of(PACK, TILE)
    square = jnp.where(row == 0, high, jnp.where(row == 1, square - high, 0.0)).astype(BF)
    for i in range(far):
        out[i, 0:rows] = own
        out[i, rows:] = square


def scale_kernel(entries, shares, grad_long, grad_short):
    rows = shares.shape[1] - PACK
    extra = shares[:, rows:].astype(F32)
    mean = jnp.sum(extra[:, :, 0:1]) / entries
    wide = jnp.broadcast_to(mean, (EDGE, TILE))
    scale = jnp.minimum(1.0, 1.0 / jnp.sqrt(wide + 1e-06))[0:1]
    total = jnp.concatenate([shares[i, 0:rows].astype(F32) for i in range(shares.shape[0])], axis=0)
    short = grad_short.shape[1]
    members = grad_short.shape[2] // grad_long.shape[0]
    per = BLOCK // members
    stride = per + 3 * (BLOCK // TILE) * EDGE
    for b in range(grad_short.shape[2] // BLOCK):
        base = b * stride
        grad_long[b * per : (b + 1) * per, :] = total[base : base + per, :] * scale
        for j in range(3):
            for h in range(BLOCK // TILE):
                at = base + per + (j * (BLOCK // TILE) + h) * EDGE
                lane = b * BLOCK + h * TILE
                grad_short[j, :, lane : lane + TILE] = total[at : at + short, :] * scale


def call(kernel, outs, scratch, *args, limit=LIMIT):
    return pl.pallas_call(
        kernel,
        in_specs=[pl.BlockSpec(memory_space=pltpu.VMEM) for _ in args],
        out_specs=[pl.BlockSpec(memory_space=pltpu.VMEM) for _ in outs],
        out_shape=[jax.ShapeDtypeStruct(s, d) for s, d in outs],
        scratch_shapes=scratch,
        compiler_params=pltpu.CompilerParams(vmem_limit_bytes=limit),
        cost_estimate=pl.CostEstimate(
            flops=2 * 10**9, bytes_accessed=8 * 10**6, transcendentals=0
        ),
    )(*args)


def step_forward(block, size):
    return lax.ppermute(block, SEQ, [(i, i + 1) for i in range(size - 1)])


def step_back(block, size):
    return lax.ppermute(block, SEQ, [(i + 1, i) for i in range(size - 1)])


def exchange(pieces, axes):
    return lax.all_to_all(pieces, axes, 0, 0)


def local(streams, short_taps, long_taps, doc_marks, upstream):
    chan, tok = streams.shape[1:]
    groups, taps = long_taps.shape
    short = short_taps.shape[2]
    members = chan // groups
    size = lax.axis_size(SEQ)
    w = jnp.transpose(short_taps, (0, 2, 1))
    marks = doc_marks.reshape(1, tok)
    shifts = ((short * tok, tok), BF)
    whole = ((3, chan, tok), BF)
    tiles = chan // TILE

    late = ((chan, TILE), BF)
    feats, next_pack, last_pack, mixed_late, gate_late = call(
        feats_kernel,
        [
            whole, ((chan + 2 * tiles * PACK, TILE), BF), ((chan + tiles * PACK, TILE), BF),
            late, late,
        ],
        [pltpu.VMEM(*shifts)],
        marks, streams, w, upstream,
        limit=FIRST_LIMIT,
    )
    from_last = step_forward(next_pack, size)
    from_next = step_back(last_pack, size)

    half = ((chan, TILE), F32)
    conv, back, part = call(
        functools.partial(own_kernel, members),
        [half, half, ((groups, taps), F32)],
        [],
        marks, mixed_late, gate_late, long_taps,
    )
    rows = groups + 3 * tiles * EDGE
    mixed_out, feat_grad, heads, sums = call(
        functools.partial(halo_kernel, members),
        [((chan, tok), BF), whole, ((3, EDGE, chan), BF), ((rows, TILE), BF)],
        [
            pltpu.VMEM(*shifts), pltpu.VMEM((BLOCK, tok), F32), pltpu.VMEM((BLOCK, tok), F32),
            pltpu.VMEM((rows, TILE), F32),
        ],
        marks, streams, w, feats, upstream, from_last, from_next, conv, back, long_taps, part,
    )
    next_heads = step_back(heads, size)

    cube = lax.axis_size(CUBE)
    tp = lax.axis_size(TP)
    far = tp * lax.axis_size("zh")
    share = rows // cube
    mine = exchange(sums.reshape(cube, share, TILE), CUBE).astype(F32)
    mine = jnp.sum(mine, axis=0).astype(BF)
    mine, feat_grad = lax.optimization_barrier((mine, feat_grad))
    pieces = exchange(jnp.broadcast_to(mine, (far,) + mine.shape), FAR)
    (grad_streams,) = call(
        streams_kernel, [whole], [pltpu.VMEM(*shifts)], marks, w, feat_grad, next_heads
    )
    pieces, grad_streams = lax.optimization_barrier((pieces, grad_streams))
    me = jnp.where(jnp.arange(tp) == lax.axis_index(TP), 1.0, 0.0).astype(F32)
    me = jnp.broadcast_to(me[:, None, None], (tp, 1, TILE))
    (payload,) = call(merge_kernel, [((cube, share + PACK, TILE), BF)], [], me, pieces)
    shares = exchange(payload, CUBE)
    entries = tp * (groups * taps + 3 * chan * short)
    grad_long, grad_short = call(
        functools.partial(scale_kernel, entries),
        [((groups, taps), F32), ((3, short, chan), F32)],
        [],
        shares,
    )
    return (mixed_out, grad_streams, grad_long, jnp.transpose(grad_short, (0, 2, 1)))


def solution(mesh):
    fine = Mesh(mesh.devices.reshape(4, 4, 4, 4, 2), ("x", "zh", "zl", "y", "c"))
    in_specs = (P(None, TP, SEQ), P(None, TP, None), P(TP, None), P(SEQ), P(TP, SEQ))
    out_specs = (P(TP, SEQ), P(None, TP, SEQ), P(TP, None), P(None, TP, None))
    return jax.shard_map(local, mesh=fine, in_specs=in_specs, out_specs=out_specs, check_vma=False)
```

```python
import functools

import jax
import jax.numpy as jnp
from jax import lax
from jax.experimental import pallas as pl
from jax.experimental.pallas import tpu as pltpu
from jax.sharding import Mesh
from jax.sharding import PartitionSpec as P

BF = jnp.bfloat16
F32 = jnp.float32
SEQ = ("x", "zh", "zl")
TP = ("y", "c")
CUBE = ("x", "zl")
FAR = ("zh", "y", "c")
TILE = 128
EDGE = 8
PACK = 16
BLOCK = 256
LIMIT = 24 * 1024 * 1024
FIRST_LIMIT = 57 * 1024 * 1024


def nt(left, right):
    return lax.dot_general(left, right, (((1,), (1,)), ((), ())), preferred_element_type=F32)


def nn(left, right):
    return lax.dot_general(left, right, (((1,), (0,)), ((), ())), preferred_element_type=F32)


def ones_where(keep):
    return jnp.where(keep, 1.0, 0.0).astype(BF)


def grid_of(rows, cols):
    return (
        lax.broadcasted_iota(jnp.int32, (rows, cols), 0),
        lax.broadcasted_iota(jnp.int32, (rows, cols), 1),
    )


def segments(marks):
    tok = marks.shape[1]
    row, col = grid_of(tok, tok)
    lower = ones_where(col <= row)
    wide = jnp.broadcast_to(jnp.where(marks[...] == 1, 1.0, 0.0), (tok, tok)).astype(BF)
    return nt(lower, wide), nt(wide, lower), row, col


def identity(size):
    row, col = grid_of(size, size)
    return ones_where(row == col)


def reversal():
    row, col = grid_of(TILE, TILE)
    return ones_where(row + col == TILE - 1)


def fill_shifts(shifts, same, offset, short):
    tok = same.shape[0]
    for lag in range(short):
        shifts[lag * tok : (lag + 1) * tok, :] = ones_where((offset == lag) & same)


def tap_columns(w, j, span):
    short = w.shape[1]
    wide = jnp.concatenate(
        [w[j, :, span], jnp.zeros((EDGE - short, BLOCK), F32)], axis=0
    )
    return jnp.transpose(wide)


def weighted(values, taps, short):
    parts = []
    values = values.astype(F32)
    for lag in range(short):
        tap = jnp.broadcast_to(taps[:, lag : lag + 1], (BLOCK, TILE))
        for lo in range(0, values.shape[1], TILE):
            parts.append((values[:, lo : lo + TILE] * tap).astype(BF))
    return jnp.concatenate(parts, axis=1)


def edge_rows(packed, first, j, lo):
    rows = []
    for h in range(BLOCK // TILE):
        slot = 3 * h + j
        at = first + (lo // BLOCK * 3 + slot // 2) * PACK
        half = slot % 2 * EDGE
        rows.append(packed[at : at + PACK, :].astype(F32)[half : half + EDGE])
    return jnp.concatenate(rows, axis=1)


def border_sum(w, j, span, pad, forward):
    total = None
    for lag in range(1, w.shape[1]):
        lo = EDGE - lag if forward else lag
        term = w[j, lag : lag + 1, span] * pad[lo : lo + EDGE]
        total = term if total is None else total + term
    return total


def after(rows):
    return jnp.concatenate([rows, jnp.zeros_like(rows)], axis=0)


def at_front(rows, eye):
    wide = jnp.concatenate([rows, jnp.zeros((TILE - EDGE, rows.shape[1]), F32)], axis=0)
    return nt(eye, wide.astype(BF))


def feats_kernel(marks, x, w, ups, feats, next_pack, last_pack, mixed_late, gate_late, shifts):
    short = w.shape[1]
    chan, tok = ups.shape
    seg_col, seg_row, row, col = segments(marks)
    fill_shifts(shifts, seg_col == seg_row, col - row, short)
    first = seg_row[0:1, :]
    open_end = first == first[:, tok - 1 : tok]
    open_start = first == 0
    head_row, head_col = grid_of(PACK, tok)
    take_tail = ones_where((head_col == tok - EDGE + head_row) & open_end & (head_row < EDGE))
    take_head = ones_where((head_col == head_row) & (head_row < EDGE) & open_start)
    for lo in range(0, chan, BLOCK):
        span = slice(lo, lo + BLOCK)
        outs = []
        tails = []
        for j in range(3):
            raw = x[j, span]
            taps = tap_columns(w, j, span)
            out = nn(weighted(raw, taps, short), shifts[...]).astype(BF)
            feats[j, span] = out
            outs.append(out.astype(F32))
            tails.append(nt(take_tail, raw)[0:EDGE])
        mixed = outs[1][:, tok - TILE :] * outs[2][:, tok - TILE :]
        mixed_late[span, :] = mixed.astype(BF)
        next_pack[span, :] = jnp.where(open_end[:, tok - TILE :], mixed, 0.0).astype(BF)
        up = ups[span]
        gate = up.astype(F32) * outs[0]
        gate_late[span, :] = gate[:, tok - TILE :].astype(BF)
        last_pack[span, :] = jnp.where(open_start[:, 0:TILE], gate[:, 0:TILE], 0.0).astype(BF)
        heads = nt(take_head, up)[0:EDGE]
        halves = [slice(h, h + TILE) for h in range(0, BLOCK, TILE)]
        block = lo // BLOCK
        at = chan + block * PACK
        last_pack[at : at + PACK, :] = jnp.concatenate(
            [heads[:, h] for h in halves], axis=0
        ).astype(BF)
        slots = [tails[j][:, h] for h in halves for j in range(3)]
        for p in range(3):
            at = chan + (block * 3 + p) * PACK
            pair = jnp.concatenate(slots[2 * p : 2 * p + 2], axis=0)
            next_pack[at : at + PACK, :] = pair.astype(BF)


def circulant(filt, g):
    row = filt[g : g + 1, :].astype(BF).astype(F32)
    wide = jnp.broadcast_to(row, (TILE, TILE))
    return pltpu.roll(wide, 0, 1, stride=1, stride_axis=0).astype(BF)


def turned_filters(filt):
    row, col = grid_of(TILE, TILE)
    return nn(filt[...].astype(BF), ones_where((row + col == TILE) | (row + col == 0)))


def spread(block, picks):
    return jnp.concatenate([block * pick for pick in picks], axis=0)


def diagonals(product):
    moved = pltpu.roll(product, 1, 1, stride=1, stride_axis=0)
    return jnp.sum(moved, axis=0, keepdims=True)


def members_mask(start, members):
    row, col = grid_of(TILE, TILE)
    return ones_where((col >= start) & (col < start + members))


def own_kernel(members, marks, mixed_late, gate_late, filt, conv, back, part):
    chan = mixed_late.shape[0]
    tok = marks.shape[1]
    seg_col, seg_row, row, col = segments(marks)
    flip = reversal()
    s = slice(TILE, tok)
    keep_bf = ones_where((seg_col[s, s] == seg_row[s, s]) & (col[s, s] >= row[s, s]))
    keep = nn(flip, keep_bf)
    keep_tbf = ones_where((seg_col[s, s] == seg_row[s, s]) & (col[s, s] <= row[s, s]))
    back_filt = turned_filters(filt)
    picks = [members_mask(p, members) for p in range(0, TILE, members)]
    for lo in range(0, chan, BLOCK):
        span = slice(lo, lo + BLOCK)
        mixed = mixed_late[span]
        gate = gate_late[span]
        mixed_t = nt(flip, mixed).astype(BF)
        for cb in range(BLOCK // TILE):
            chans = slice(cb * TILE, (cb + 1) * TILE)
            products = nn(spread(mixed_t[:, chans], picks), gate[chans])
            for k in range(len(picks)):
                g = cb * len(picks) + k
                n = lo // members + g
                rows = slice(g * members, (g + 1) * members)
                at = slice(lo + g * members, lo + (g + 1) * members)
                conv[at, :] = nn(mixed[rows], circulant(filt, n) * keep_bf)
                back[at, :] = nn(gate[rows], circulant(back_filt, n) * keep_tbf)
                part[n : n + 1, :] = diagonals(products[k * TILE : (k + 1) * TILE] * keep)


def halo_kernel(
    members, marks, x, w, feats, ups, from_last, from_next, conv, back, filt, part,
    mixed_out, grads, heads, sums_out, shifts, conv_s, back_s, sums,
):
    short = w.shape[1]
    chan, tok = ups.shape
    seg_col, seg_row, row, col = segments(marks)
    fill_shifts(shifts, seg_col == seg_row, col - row, short)
    eye = identity(BLOCK)
    flip = reversal()
    first = seg_row[0:1, :]
    middle = first[:, TILE - 1 : TILE]
    last = first[:, tok - 1 : tok]
    from_start = [
        jnp.where(first[:, 0:TILE] == 0, 1.0, 0.0),
        jnp.where(first[:, TILE:] == middle, 1.0, 0.0),
    ]
    to_end = [
        jnp.where(first[:, 0:TILE] == middle, 1.0, 0.0),
        jnp.where(first[:, TILE:] == last, 1.0, 0.0),
    ]
    row_t, col_t = grid_of(TILE, TILE)
    upper_bf = ones_where(col_t < row_t)
    upper = jnp.where(col_t + row_t < TILE - 1, 1.0, 0.0)
    s = slice(0, TILE)
    keep_bf = ones_where((seg_col[s, s] == seg_row[s, s]) & (col[s, s] >= row[s, s]))
    keep = nn(flip, keep_bf)
    keep_tbf = ones_where((seg_col[s, s] == seg_row[s, s]) & (col[s, s] <= row[s, s]))
    upper_tbf = ones_where(col_t > row_t)
    back_filt = turned_filters(filt)
    open_start = seg_col[0:EDGE, 0:BLOCK] == 0
    head_row, head_col = grid_of(EDGE, tok)
    take_head = ones_where((head_col == head_row) & (first == 0))
    take_tail = ones_where((head_col == tok - EDGE + head_row) & (first == last))
    picks = [members_mask(p, members) for p in range(0, TILE, members)]
    per = BLOCK // members
    stride = per + 3 * (BLOCK // TILE) * EDGE
    for lo in range(0, chan, BLOCK):
        span = slice(lo, lo + BLOCK)
        pads = [after(edge_rows(from_last, chan, j, lo)) for j in range(3)]
        feat = []
        for j in range(3):
            fix = jnp.where(open_start, border_sum(w, j, span, pads[j], True), 0.0)
            head = (feats[j, span, 0:TILE].astype(F32) + at_front(fix, eye)).astype(BF)
            feat.append(jnp.concatenate([head, feats[j, span, TILE:]], axis=1).astype(F32))
        up = ups[span].astype(F32)
        gate = up * feat[0]
        mixed = feat[1][:, 0:TILE] * feat[2][:, 0:TILE]
        mixed_b = mixed.astype(BF)
        gate_b = gate[:, 0:TILE].astype(BF)
        mixed0 = (mixed * to_end[0]).astype(BF)
        gate0 = (gate[:, 0:TILE] * from_start[0]).astype(BF)
        gate1 = (gate[:, TILE:] * from_start[1]).astype(BF)
        mixed_h = from_last[span]
        beyond = border_sum(w, 0, span, after(nt(take_tail, x[0, span])), True)
        at = chan + lo // BLOCK * PACK
        packed = from_next[at : at + PACK, :].astype(F32)
        ups_head = jnp.concatenate([packed[0:EDGE], packed[EDGE:]], axis=1)
        gate_h = (from_next[span].astype(F32) + at_front(ups_head * beyond, eye)).astype(BF)
        lead_t = nt(flip, mixed_h).astype(BF)
        mixed_t = nt(flip, mixed0).astype(BF)
        whole_t = nt(flip, mixed_b).astype(BF)
        base = lo // BLOCK * stride
        for cb in range(BLOCK // TILE):
            chans = slice(cb * TILE, (cb + 1) * TILE)
            both = jnp.concatenate(
                [spread(lead_t[:, chans], picks), spread(mixed_t[:, chans], picks)], axis=1
            )
            products = nn(both, jnp.concatenate([gate0[chans], gate1[chans]], axis=0))
            inners = nn(spread(whole_t[:, chans], picks), gate_b[chans])
            for k in range(len(picks)):
                g = cb * len(picks) + k
                n = lo // members + g
                table = circulant(filt, n)
                diag = table * keep_bf
                table = table * upper_bf
                turned = circulant(back_filt, n)
                diag_b = turned * keep_tbf
                turned = turned * upper_tbf
                rows = slice(g * members, (g + 1) * members)
                at = slice(lo + g * members, lo + (g + 1) * members)
                ahead = nn(
                    jnp.concatenate([mixed_h[rows], mixed0[rows], mixed_b[rows]], axis=0),
                    jnp.concatenate([table, diag], axis=1),
                )
                conv_s[rows, 0:TILE] = (
                    ahead[2 * members :, TILE:] + ahead[0:members, 0:TILE] * from_start[0]
                )
                conv_s[rows, TILE:] = (
                    conv[at] + ahead[members : 2 * members, 0:TILE] * from_start[1]
                )
                behind = nn(
                    jnp.concatenate([gate1[rows], gate_h[rows], gate_b[rows]], axis=0),
                    jnp.concatenate([turned, diag_b], axis=1),
                )
                back_s[rows, 0:TILE] = (
                    behind[2 * members :, TILE:] + behind[0:members, 0:TILE] * to_end[0]
                )
                back_s[rows, TILE:] = (
                    back[at] + behind[members : 2 * members, 0:TILE] * to_end[1]
                )
                spots = slice(k * TILE, (k + 1) * TILE)
                sums[base + g : base + g + 1, :] = part[n : n + 1, :] + diagonals(
                    products[spots] * upper + inners[spots] * keep
                )
        conv_v = conv_s[...]
        back_v = back_s[...]
        mixed_out[span, :] = (feat[0] * conv_v).astype(BF)
        grad = [
            (up * conv_v).astype(BF),
            (back_v * feat[2]).astype(BF),
            (back_v * feat[1]).astype(BF),
        ]
        for j in range(3):
            grads[j, span] = grad[j]
            moved = nt(shifts[...], grad[j])
            raw = nt(eye, x[j, span])
            head = nt(take_head, grad[j])
            heads[j, :, span] = head.astype(BF)
            columns = []
            for lag in range(short):
                piece = moved[lag * tok : (lag + 1) * tok]
                column = jnp.sum(raw * piece, axis=0, keepdims=True)
                if lag > 0:
                    cross = head * pads[j][EDGE - lag : 2 * EDGE - lag]
                    column = column + jnp.sum(cross, axis=0, keepdims=True)
                columns.append(column)
            columns += [jnp.zeros((1, BLOCK), F32)] * (EDGE - short)
            stacked = jnp.concatenate(columns, axis=0)
            for h in range(BLOCK // TILE):
                at = base + per + (j * (BLOCK // TILE) + h) * EDGE
                sums[at : at + EDGE, :] = stacked[:, h * TILE : (h + 1) * TILE]
    sums_out[...] = sums[...].astype(BF)


def streams_kernel(marks, w, grads, next_heads, out, shifts):
    short = w.shape[1]
    tok = marks.shape[1]
    seg_col, seg_row, row, col = segments(marks)
    fill_shifts(shifts, seg_col == seg_row, row - col, short)
    open_end = seg_col[tok - EDGE :, 0:BLOCK] == seg_col[tok - 1 : tok, 0:BLOCK]
    eye = identity(BLOCK)
    for lo in range(0, grads.shape[1], BLOCK):
        span = slice(lo, lo + BLOCK)
        for j in range(3):
            taps = tap_columns(w, j, span)
            total = nn(weighted(grads[j, span], taps, short), shifts[...])
            pad = next_heads[j, :, span].astype(F32)
            pad = jnp.concatenate([jnp.zeros_like(pad), pad], axis=0)
            fix = jnp.where(open_end, border_sum(w, j, span, pad, False), 0.0)
            wide = jnp.concatenate([jnp.zeros((TILE - EDGE, BLOCK), F32), fix], axis=0)
            out[j, span, 0:TILE] = total[:, 0:TILE].astype(BF)
            out[j, span, TILE:] = (total[:, TILE:] + nt(eye, wide.astype(BF))).astype(BF)


def merge_kernel(me, pieces, out):
    far = out.shape[0]
    tp = me.shape[0]
    rows = pieces.shape[1]
    rest = pieces.shape[0] // tp
    total = pieces[0:tp].astype(F32)
    for z in range(1, rest):
        total = total + pieces[z * tp : (z + 1) * tp].astype(F32)
    own = jnp.sum(total * me[...], axis=0).astype(BF)
    square = jnp.broadcast_to(jnp.sum(total * total), (PACK, TILE))
    high = square.astype(BF).astype(F32)
    row, _ = grid_of(PACK, TILE)
    square = jnp.where(row == 0, high, jnp.where(row == 1, square - high, 0.0)).astype(BF)
    for i in range(far):
        out[i, 0:rows] = own
        out[i, rows:] = square


def scale_kernel(entries, shares, grad_long, grad_short):
    rows = shares.shape[1] - PACK
    extra = shares[:, rows:].astype(F32)
    mean = jnp.sum(extra[:, :, 0:1]) / entries
    wide = jnp.broadcast_to(mean, (EDGE, TILE))
    scale = jnp.minimum(1.0, 1.0 / jnp.sqrt(wide + 1e-06))[0:1]
    total = jnp.concatenate([shares[i, 0:rows].astype(F32) for i in range(shares.shape[0])], axis=0)
    short = grad_short.shape[1]
    members = grad_short.shape[2] // grad_long.shape[0]
    per = BLOCK // members
    stride = per + 3 * (BLOCK // TILE) * EDGE
    for b in range(grad_short.shape[2] // BLOCK):
        base = b * stride
        grad_long[b * per : (b + 1) * per, :] = total[base : base + per, :] * scale
        for j in range(3):
            for h in range(BLOCK // TILE):
                at = base + per + (j * (BLOCK // TILE) + h) * EDGE
                lane = b * BLOCK + h * TILE
                grad_short[j, :, lane : lane + TILE] = total[at : at + short, :] * scale


def call(kernel, outs, scratch, *args, limit=LIMIT):
    return pl.pallas_call(
        kernel,
        in_specs=[pl.BlockSpec(memory_space=pltpu.VMEM) for _ in args],
        out_specs=[pl.BlockSpec(memory_space=pltpu.VMEM) for _ in outs],
        out_shape=[jax.ShapeDtypeStruct(s, d) for s, d in outs],
        scratch_shapes=scratch,
        compiler_params=pltpu.CompilerParams(vmem_limit_bytes=limit),
        cost_estimate=pl.CostEstimate(
            flops=2 * 10**9, bytes_accessed=8 * 10**6, transcendentals=0
        ),
    )(*args)


def step_forward(block, size):
    return lax.ppermute(block, SEQ, [(i, i + 1) for i in range(size - 1)])


def step_back(block, size):
    return lax.ppermute(block, SEQ, [(i + 1, i) for i in range(size - 1)])


def exchange(pieces, axes):
    return lax.all_to_all(pieces, axes, 0, 0)


def local(streams, short_taps, long_taps, doc_marks, upstream):
    chan, tok = streams.shape[1:]
    groups, taps = long_taps.shape
    short = short_taps.shape[2]
    members = chan // groups
    size = lax.axis_size(SEQ)
    w = jnp.transpose(short_taps, (0, 2, 1))
    marks = doc_marks.reshape(1, tok)
    shifts = ((short * tok, tok), BF)
    whole = ((3, chan, tok), BF)
    tiles = chan // TILE
    blocks = chan // BLOCK

    late = ((chan, TILE), BF)
    feats, next_pack, last_pack, mixed_late, gate_late = call(
        feats_kernel,
        [
            whole, ((chan + 3 * blocks * PACK, TILE), BF), ((chan + blocks * PACK, TILE), BF),
            late, late,
        ],
        [pltpu.VMEM(*shifts)],
        marks, streams, w, upstream,
        limit=FIRST_LIMIT,
    )
    from_last = step_forward(next_pack, size)
    from_next = step_back(last_pack, size)

    half = ((chan, TILE), F32)
    conv, back, part = call(
        functools.partial(own_kernel, members),
        [half, half, ((groups, taps), F32)],
        [],
        marks, mixed_late, gate_late, long_taps,
    )
    rows = groups + 3 * tiles * EDGE
    mixed_out, feat_grad, heads, sums = call(
        functools.partial(halo_kernel, members),
        [((chan, tok), BF), whole, ((3, EDGE, chan), BF), ((rows, TILE), BF)],
        [
            pltpu.VMEM(*shifts), pltpu.VMEM((BLOCK, tok), F32), pltpu.VMEM((BLOCK, tok), F32),
            pltpu.VMEM((rows, TILE), F32),
        ],
        marks, streams, w, feats, upstream, from_last, from_next, conv, back, long_taps, part,
    )
    next_heads = step_back(heads, size)

    cube = lax.axis_size(CUBE)
    tp = lax.axis_size(TP)
    far = tp * lax.axis_size("zh")
    share = rows // cube
    mine = exchange(sums.reshape(cube, share, TILE), CUBE).astype(F32)
    mine = jnp.sum(mine, axis=0).astype(BF)
    mine, feat_grad = lax.optimization_barrier((mine, feat_grad))
    pieces = exchange(jnp.broadcast_to(mine, (far,) + mine.shape), FAR)
    (grad_streams,) = call(
        streams_kernel, [whole], [pltpu.VMEM(*shifts)], marks, w, feat_grad, next_heads
    )
    pieces, grad_streams = lax.optimization_barrier((pieces, grad_streams))
    me = jnp.where(jnp.arange(tp) == lax.axis_index(TP), 1.0, 0.0).astype(F32)
    me = jnp.broadcast_to(me[:, None, None], (tp, 1, TILE))
    (payload,) = call(merge_kernel, [((cube, share + PACK, TILE), BF)], [], me, pieces)
    shares = exchange(payload, CUBE)
    entries = tp * (groups * taps + 3 * chan * short)
    grad_long, grad_short = call(
        functools.partial(scale_kernel, entries),
        [((groups, taps), F32), ((3, short, chan), F32)],
        [],
        shares,
    )
    return (mixed_out, grad_streams, grad_long, jnp.transpose(grad_short, (0, 2, 1)))


def solution(mesh):
    fine = Mesh(mesh.devices.reshape(4, 4, 4, 4, 2), ("x", "zh", "zl", "y", "c"))
    in_specs = (P(None, TP, SEQ), P(None, TP, None), P(TP, None), P(SEQ), P(TP, SEQ))
    out_specs = (P(TP, SEQ), P(None, TP, SEQ), P(TP, None), P(None, TP, None))
    return jax.shard_map(local, mesh=fine, in_specs=in_specs, out_specs=out_specs, check_vma=False)
```
